128 devices in a mesh: aa: 4 (over z), ba: 32 (over y, x, core).
Axes of the slice: x: 4, y: 4, z: 4, core: 2. Of those that a mesh axis runs over, the one named last changes fastest.
Arguments:
- features: bfloat16 [32, 524288], P(None, ('aa', 'ba')), may hold values from -6 to 6
- cotangent: bfloat16 [32, 524288], P(None, ('aa', 'ba')), may hold values from -6 to 6
- owner: int32 [524288, 1], P(('aa', 'ba')), may hold values from 0 to 127; in each aligned block of 4096 rows (0 to 4095, 4096 to 8191, ...) at most 128 rows name the same one
- offset: bfloat16 [3, 524288], P(None, ('aa', 'ba')), may hold values from 0 to 0.98828125
- kernel_one: bfloat16 [27, 32, 32], replicated, may hold values from -0.21875 to 0.21875
- kernel_two: bfloat16 [27, 32, 32], replicated, may hold values from -0.21875 to 0.21875
- mlp_in: bfloat16 [128, 32], replicated, may hold values from -1 to 1
- mlp_out: bfloat16 [32, 128], replicated, may hold values from -0.5 to 0.5
Outputs:
- particle_out: bfloat16 [32, 524288], P(None, ('aa', 'ba'))
- feat_grad: bfloat16 [32, 524288], P(None, ('aa', 'ba'))
- kernel_grads: float32 [2, 27, 32, 32], replicated
- grad_mlp_in: float32 [128, 32], replicated
- grad_mlp_out: float32 [32, 128], replicated
The draws below stay inside these ranges and needn't reach their ends.
Inputs may be any that keep to these rules, and one draw needn't show every extreme that they name: Among the particles of one device at most 128 have the same owner, and in some devices' particles one owner has exactly 128.
All inputs are finite; a program needn't handle non-finite values.
Results may differ from the reference program's by a relative error of at most 0.0056.
Values may be sent and summed in bfloat16 or wider, within the bound.
No kernel may reach another device: no remote copies, remote signals or barrier semaphores. Data moves between devices by JAX's collectives and lax.ppermute only.
A program may use at most 192 MiB of HBM per device.

```python
import math
import jax
import jax.numpy as jnp
import numpy as np
from jax import lax

C = 32
H = 128
GZ = 64
CXD = 4
CYD = 32
PART_DEV = 4096
CAP = 128
GX = 128
GY = 128
PARTICLES = 524288
N_BA = 32
DEVICES = 128


def steps_of(key, shape, pieces, least, top_value):
    level, own = 1.0, jax.random.fold_in(key, 6)
    for axis_at, shards_of in pieces:
        heights = jnp.exp(jax.random.uniform(jax.random.fold_in(own, axis_at), (shards_of,), jnp.float32, least / len(pieces), top_value / len(pieces)))
        level = level * jnp.repeat(heights, shape[axis_at] // shards_of).reshape([-1 if axis == axis_at else 1 for axis in range(len(shape))])
    return level


def assign_block(key, own, number, rows, amount, top, limit, skew):
    sequence = jax.random.permutation(key, amount)
    packed, ordinary = portions_of(amount, rows * top, limit, skew, True), portions_of(amount, rows * top, limit, skew, False)
    places = jnp.arange(amount)

    def named(lengths, offset_by):
        used = int((lengths > 0).sum())
        fixed = max(1, used // 4)
        passed = fixed + (places - fixed + offset_by * (used - fixed)) % max(1, amount - fixed)
        return jnp.zeros((amount,), jnp.int32).at[sequence[jnp.where(places < fixed, places, passed)]].set(jnp.asarray(lengths, jnp.int32))

    lengths = jnp.where(number % 4 == 0, named(packed, number // 4), named(ordinary, number - number // 4 - 1))
    mixed = jax.random.permutation(jax.random.fold_in(own, 3), amount)
    donor, taker = mixed[0:amount // 2 * 2:2], mixed[1:amount // 2 * 2:2]
    room = jnp.minimum(lengths[donor] - 1, limit - lengths[taker]) // 2
    room = jnp.where((donor == sequence[0]) | (taker == sequence[0]) | (lengths[taker] == 0), 0, jnp.maximum(room, 0))
    passed = jax.random.randint(jax.random.fold_in(own, 4), (amount // 2,), 0, 1 << 20) % (room + 1)
    lengths = lengths.at[donor].add(-passed).at[taker].add(passed)
    members = jnp.searchsorted(jnp.cumsum(lengths), jnp.arange(rows * top), side="right").astype(jnp.int32)
    table = members.reshape(top, rows).T
    table = table[jax.random.permutation(jax.random.fold_in(own, 1), rows)]
    offset_by = jax.random.randint(jax.random.fold_in(own, 2), (rows, 1), 0, top)
    return jnp.take_along_axis(table, (jnp.arange(top)[None, :] + offset_by) % top, axis=1)


def portions_of(count, total, most, slope, full):
    loads = [(1 << 20) // math.isqrt(standing ** slope) + 1 for standing in range(1, count + 1)]
    largest = most if full else min(most, max(-(-total // count), total * loads[0] // sum(loads)))
    least = 1 if total - largest >= count - 1 else 0
    holding, rest = [largest] + [least] * (count - 1), total - largest - least * (count - 1)
    while rest > 0:
        candidates = [i for i in range(1, count) if holding[i] < largest] or [i for i in range(1, count) if holding[i] < most]
        whole, remaining = sum([loads[i] for i in candidates]), rest
        for i in candidates:
            addition = min(most - holding[i], max(1, remaining * loads[i] // whole), rest)
            holding[i] = holding[i] + addition
            rest = rest - addition
    return np.array(holding)


def scatter_about(own_key, shape, width, limit, cuts=(), kind=jnp.bfloat16):
    entries = jax.random.normal(own_key, shape, jnp.float32) * width
    if len(cuts) > 0:
        entries = steps_of(own_key, shape, cuts, -0.22, 0.18) * entries
    return jnp.clip(entries, min=-limit, max=limit).astype(kind)


def setup_inputs(seed: int = 0) -> dict:
    key_list = jax.random.split(jax.random.key(seed), 9)
    features = scatter_about(key_list[0], (C, PARTICLES), 1.0, 6.0, ((1, 128),))
    cotangent = scatter_about(key_list[1], (C, PARTICLES), 1.0, 6.0, ((1, 128),))
    owner_keys = jax.random.split(jax.random.fold_in(key_list[2], 1), PARTICLES // PART_DEV)
    owner_turns = jax.random.permutation(jax.random.fold_in(key_list[2], 3), PARTICLES // PART_DEV)
    owner = jax.vmap(lambda own, number: assign_block(jax.random.fold_in(key_list[2], 2), own, number, PART_DEV, DEVICES, 1, CAP, 2))(owner_keys, owner_turns).reshape((PARTICLES, 1))
    offset = jnp.clip(0.98828125 * jax.random.uniform(key_list[3], (3, PARTICLES), jnp.float32) ** steps_of(key_list[3], (3, PARTICLES), ((1, 128),), -0.2, 0.2), 0.0, 0.98828125).astype(jnp.bfloat16)
    kernel_one = scatter_about(key_list[4], (27, C, C), (27 * C) ** -0.5, 0.21875)
    kernel_two = scatter_about(key_list[5], (27, C, C), (27 * C) ** -0.5, 0.21875)
    mlp_in = scatter_about(key_list[6], (H, C), C ** -0.5, 1.0)
    mlp_out = scatter_about(key_list[7], (C, H), H ** -0.5, 0.5)
    return {"features": features, "cotangent": cotangent, "owner": owner, "offset": offset, "kernel_one": kernel_one, "kernel_two": kernel_two, "mlp_in": mlp_in, "mlp_out": mlp_out}


def shift_list():
    return [(step_x, step_y, step_z) for step_x in (-1, 0, 1) for step_y in (-1, 0, 1) for step_z in (-1, 0, 1)]


def silu_slope(value):
    sigma_value = jax.nn.sigmoid(value)
    return sigma_value * (1.0 + value * (1.0 - sigma_value))


def flipped(kernel):
    return jnp.transpose(kernel[::-1], (0, 2, 1))


def corner_weights(offset, owner):
    scale = jnp.array([CXD - 1, CYD - 1, GZ - 1], dtype=jnp.float32)
    position = offset.astype(jnp.float32) * scale[:, None]
    corner_base = jnp.floor(position)
    fraction = position - corner_base
    cell_index = corner_base.astype(jnp.int32)
    owners = owner[:, 0].astype(jnp.int32)
    grid_x = (owners % N_BA) * CXD + cell_index[0]
    grid_y = (owners // N_BA) * CYD + cell_index[1]
    result = []
    for step_x in (0, 1):
        for step_y in (0, 1):
            for step_z in (0, 1):
                flat_index = ((grid_x + step_x) * GY + grid_y + step_y) * GZ + cell_index[2] + step_z
                factor_x = fraction[0] if step_x else 1.0 - fraction[0]
                factor_y = fraction[1] if step_y else 1.0 - fraction[1]
                factor_z = fraction[2] if step_z else 1.0 - fraction[2]
                result.append((flat_index.astype(jnp.int32), factor_x * factor_y * factor_z))
    return result


def to_grid(values, corners):
    grid_flat = jnp.zeros((values.shape[0], GX * GY * GZ), jnp.float32)
    wide_values = values.astype(jnp.float32)
    for flat_index, factor in corners:
        grid_flat = grid_flat.at[:, flat_index].add(wide_values * factor[None, :])
    return grid_flat


def from_grid(grid_flat, corners):
    summed = None
    for flat_index, factor in corners:
        product = grid_flat[:, flat_index].astype(jnp.float32) * factor[None, :]
        summed = product if summed is None else summed + product
    return summed


def convolve(field, kernel):
    padded = jnp.pad(field, ((0, 0), (1, 1), (1, 1), (1, 1)))
    weights = kernel.astype(jnp.float32)

    def one_plane(slab):
        block = lax.dynamic_slice_in_dim(padded, slab, 3, 1).astype(jnp.float32)
        summed = jnp.zeros((weights.shape[1], GY, GZ), jnp.float32)
        for number, (step_x, step_y, step_z) in enumerate(shift_list()):
            window = block[:, step_x + 1, 1 + step_y:1 + step_y + GY, 1 + step_z:1 + step_z + GZ]
            summed = summed + jnp.einsum("oi,iyz->oyz", weights[number], window)
        return summed

    planes = lax.map(one_plane, jnp.arange(GX, dtype=jnp.int32))
    return jnp.moveaxis(planes, 0, 1)


def kernel_gradient(upstream, field):
    padded = jnp.pad(field, ((0, 0), (1, 1), (1, 1), (1, 1)))

    def one_step(carried, slab):
        block = lax.dynamic_slice_in_dim(padded, slab, 3, 1).astype(jnp.float32)
        layer = lax.dynamic_index_in_dim(upstream, slab, 1, keepdims=False).astype(jnp.float32)
        updates = []
        for step_x, step_y, step_z in shift_list():
            window = block[:, step_x + 1, 1 + step_y:1 + step_y + GY, 1 + step_z:1 + step_z + GZ]
            updates.append(jnp.einsum("oyz,iyz->oi", layer, window))
        return carried + jnp.stack(updates), None

    summed, unused_out = lax.scan(one_step, jnp.zeros((27, C, C), jnp.float32), jnp.arange(GX, dtype=jnp.int32))
    return summed


def reference(features, cotangent, owner, offset, kernel_one, kernel_two, mlp_in, mlp_out):
    corners = corner_weights(offset, owner)
    grid_zero = to_grid(features, corners).astype(jnp.bfloat16).reshape(C, GX, GY, GZ)
    pre_one = convolve(grid_zero, kernel_one)
    act_one = jax.nn.silu(pre_one).astype(jnp.bfloat16)
    grid_one = (grid_zero.astype(jnp.float32) + convolve(act_one, kernel_two)).astype(jnp.bfloat16)
    sampled = from_grid(grid_one.reshape(C, GX * GY * GZ), corners).astype(jnp.bfloat16)
    sampled = lax.optimization_barrier(sampled)
    hidden_pre = jnp.dot(mlp_in, features, preferred_element_type=jnp.float32)
    hidden = jax.nn.silu(hidden_pre).astype(jnp.bfloat16)
    local_out = jnp.dot(mlp_out, hidden, preferred_element_type=jnp.float32)
    particle_out = (sampled.astype(jnp.float32) + local_out).astype(jnp.bfloat16)

    grad_mlp_out = jnp.dot(cotangent, hidden.T, preferred_element_type=jnp.float32)
    hidden_back = jnp.dot(mlp_out.T, cotangent, preferred_element_type=jnp.float32)
    pre_grad = (hidden_back * silu_slope(hidden_pre)).astype(jnp.bfloat16)
    grad_mlp_in = jnp.dot(pre_grad, features.T, preferred_element_type=jnp.float32)
    local_back = jnp.dot(mlp_in.T, pre_grad, preferred_element_type=jnp.float32)

    back_one = to_grid(cotangent, corners).astype(jnp.bfloat16).reshape(C, GX, GY, GZ)
    act_back = convolve(back_one, flipped(kernel_two))
    pre_back = (act_back * silu_slope(pre_one)).astype(jnp.bfloat16)
    back_zero = (back_one.astype(jnp.float32) + convolve(pre_back, flipped(kernel_one))).astype(jnp.bfloat16)
    kernel_grads = jnp.stack([kernel_gradient(pre_back, grid_zero), kernel_gradient(back_one, act_one)])
    particle_back = from_grid(back_zero.reshape(C, GX * GY * GZ), corners).astype(jnp.bfloat16)
    particle_back = lax.optimization_barrier(particle_back)
    feat_grad = (particle_back.astype(jnp.float32) + local_back).astype(jnp.bfloat16)
    return particle_out, feat_grad, kernel_grads, grad_mlp_in, grad_mlp_out
```

```python
import functools

import jax
import jax.numpy as jnp
from jax import lax
from jax.experimental import pallas as pl
from jax.experimental.pallas import tpu as pltpu
from jax.sharding import PartitionSpec as P

F32 = jnp.float32
BF16 = jnp.bfloat16
NT = (((1,), (1,)), ((), ()))

DEVICES = 128
SLOTS = 128
PARTICLES = 4096
CHANNELS = 32
GZ = 64
CXD = 4
CYD = 32
PLANE = CYD * GZ
ROWS = 72
GROUP = 80
LOW = 16
HIGH = DEVICES // LOW
VMEM_LIMIT = 56 * 2**20


def params():
    return pltpu.CompilerParams(vmem_limit_bytes=VMEM_LIMIT)


def cost(macs, moved):
    return pl.CostEstimate(flops=2 * macs, bytes_accessed=moved, transcendentals=0)


def rows16(row):
    return jnp.broadcast_to(row, (16, row.shape[1]))


def silu_slope(value):
    sigma_value = jax.nn.sigmoid(value)
    return sigma_value * (1.0 + value * (1.0 - sigma_value))


def flipped(kernel):
    return jnp.transpose(kernel[::-1], (0, 2, 1))


def route_kernel(owner_ref, payload_ref, out_ref, slot_ref, spread):
    block = 256
    owner_ids = lax.broadcasted_iota(jnp.int32, (DEVICES, block), 0)
    before = lax.broadcasted_iota(jnp.int32, (block, block + 128), 0)
    after = lax.broadcasted_iota(jnp.int32, (block, block + 128), 1)
    prefix = ((before < after) | (after >= block)).astype(F32).astype(BF16)
    base = jnp.zeros((DEVICES, 128), F32)
    ranks = []
    for number in range(PARTICLES // block):
        hot = (owner_ids == owner_ref[:, number * block : (number + 1) * block]).astype(F32)
        counted = jnp.dot(hot.astype(BF16), prefix, preferred_element_type=F32)
        earlier = counted[:, :block] + jnp.concatenate([base, base], axis=1)
        ranks.append(jnp.sum(hot * earlier, axis=0, keepdims=True))
        base = base + counted[:, block:]
    rank = jnp.concatenate(ranks, axis=1).astype(jnp.int32)
    owner = owner_ref[...]
    low = lax.rem(owner, LOW)
    slot = lax.div(owner, LOW) * SLOTS + rank
    slot_ref[...] = slot
    for group in range(LOW):
        mask = rows16((low == group).astype(F32)).astype(BF16)
        for part in range(GROUP // 16):
            spread[group * GROUP + part * 16 : group * GROUP + part * 16 + 16, :] = (
                payload_ref[part * 16 : part * 16 + 16, :] * mask
            )
    width = 256
    for step in range(HIGH * SLOTS // width):
        slot_ids = lax.broadcasted_iota(jnp.int32, (width, PARTICLES), 0) + step * width
        hot = (slot_ids == slot).astype(F32).astype(BF16)
        placed = lax.dot_general(spread[...], hot, NT, preferred_element_type=F32)
        for part in range(width // SLOTS):
            high = step * (width // SLOTS) + part
            for group in range(LOW):
                out_ref[high * LOW + group] = placed[
                    group * GROUP : group * GROUP + ROWS, part * SLOTS : (part + 1) * SLOTS
                ].astype(BF16)


def route(owner, payload):
    return pl.pallas_call(
        route_kernel,
        out_shape=(
            jax.ShapeDtypeStruct((DEVICES, ROWS, SLOTS), BF16),
            jax.ShapeDtypeStruct((1, PARTICLES), jnp.int32),
        ),
        scratch_shapes=[pltpu.VMEM((LOW * GROUP, PARTICLES), BF16)],
        compiler_params=params(),
        cost_estimate=cost(LOW * GROUP * PARTICLES * HIGH * SLOTS, 3 * 2**20),
    )(owner, payload)


def network_kernel(feat_ref, cot_ref, in_ref, out_ref, in_t_ref, out_t_ref, local_ref, back_ref, grads_ref):
    step = pl.program_id(0)
    features = feat_ref[...]
    cotangent = cot_ref[...]
    hidden_pre = jnp.dot(in_ref[...], features, preferred_element_type=F32)
    hidden = jax.nn.silu(hidden_pre).astype(BF16)
    local_ref[...] = jnp.dot(out_ref[...], hidden, preferred_element_type=F32)
    hidden_back = jnp.dot(out_t_ref[...], cotangent, preferred_element_type=F32)
    pre_grad = (hidden_back * silu_slope(hidden_pre)).astype(BF16)
    back_ref[...] = jnp.dot(in_t_ref[...], pre_grad, preferred_element_type=F32)
    grad_in = lax.dot_general(features, pre_grad, NT, preferred_element_type=F32)
    grad_out = lax.dot_general(cotangent, hidden, NT, preferred_element_type=F32)
    both = jnp.concatenate([grad_in, grad_out], axis=0)

    @pl.when(step == 0)
    def first():
        grads_ref[...] = both

    @pl.when(step > 0)
    def later():
        grads_ref[...] += both


def network(features, cotangent, mlp_in, mlp_out):
    width = 1024
    hidden = mlp_in.shape[0]

    def whole(rows, columns):
        return pl.BlockSpec((rows, columns), lambda i: (0, 0))

    wide = pl.BlockSpec((CHANNELS, width), lambda i: (0, i))
    return pl.pallas_call(
        network_kernel,
        grid=(PARTICLES // width,),
        in_specs=[
            wide,
            wide,
            whole(hidden, CHANNELS),
            whole(CHANNELS, hidden),
            whole(CHANNELS, hidden),
            whole(hidden, CHANNELS),
        ],
        out_specs=(wide, wide, whole(2 * CHANNELS, hidden)),
        out_shape=(
            jax.ShapeDtypeStruct((CHANNELS, PARTICLES), F32),
            jax.ShapeDtypeStruct((CHANNELS, PARTICLES), F32),
            jax.ShapeDtypeStruct((2 * CHANNELS, hidden), F32),
        ),
        compiler_params=params(),
        cost_estimate=cost(6 * 128 * 128 * PARTICLES, 2 * 2**20),
    )(features, cotangent, mlp_in, mlp_out, mlp_in.T, mlp_out.T)


def hat(position, at):
    return jnp.maximum(1.0 - jnp.abs(position - at), 0.0)


def places(offset):
    pos_x = offset[0:1] * float(CXD - 1)
    pos_y = jnp.broadcast_to(offset[1:2] * float(CYD - 1), (8, SLOTS))
    pos_z = offset[2:3] * float(GZ - 1)
    depth = lax.broadcasted_iota(jnp.int32, (GZ, SLOTS), 0).astype(F32)
    return pos_x, pos_y, hat(pos_z, depth)


def plane_weights(pos_y, weight_z, first, count):
    rows = []
    for y in range(first, first + count):
        weight_y = hat(pos_y, float(y))
        for part in range(GZ // 8):
            rows.append(weight_y * weight_z[part * 8 : part * 8 + 8])
    return jnp.concatenate(rows, axis=0).astype(BF16)


def scatter_kernel(
    blocks, in_ref, out_ref, head_x, tail_x, head_y, tail_y, hh, ht, th, tt, total
):
    step = pl.program_id(0)
    lines = 4
    sources, placed = [], []
    for j in range(blocks):
        pos_x, pos_y, weight_z = places(in_ref[j, 64:72, :].astype(F32))
        placed.append((pos_y, weight_z))
        parts = []
        for field in range(2):
            values = in_ref[j, field * CHANNELS : (field + 1) * CHANNELS, :].astype(F32)
            for x in range(CXD):
                parts.append((values * hat(pos_x, float(x))).astype(BF16))
        sources.append(jnp.concatenate(parts, axis=0))
    source = jnp.concatenate(sources, axis=1)

    @pl.when(step == 0)
    def first():
        total[...] = jnp.zeros_like(total)

    for y in range(0, CYD, lines):
        weights = jnp.concatenate([plane_weights(*place, y, lines) for place in placed], axis=1)
        total[:, y * GZ : (y + lines) * GZ] += lax.dot_general(
            source, weights, NT, preferred_element_type=F32
        )

    @pl.when(step == pl.num_programs(0) - 1)
    def last():
        rows = CXD * CHANNELS
        edge = 2 * GZ
        for field in range(2):
            cells = total[field * rows : (field + 1) * rows].astype(BF16)
            head, tail = cells[: rows // 2], cells[rows // 2 :]
            out_ref[field] = cells
            head_x[field] = head
            tail_x[field] = tail
            head_y[field] = cells[:, :edge]
            tail_y[field] = cells[:, PLANE - edge :]
            hh[field] = head[:, :edge]
            ht[field] = head[:, PLANE - edge :]
            th[field] = tail[:, :edge]
            tt[field] = tail[:, PLANE - edge :]


def scatter(arrived):
    blocks = 16
    rows = CXD * CHANNELS
    shapes = [(rows, PLANE)] + [(rows // 2, PLANE)] * 2 + [(rows, 2 * GZ)] * 2
    shapes = [(2,) + shape for shape in shapes + [(rows // 2, 2 * GZ)] * 4]
    return pl.pallas_call(
        functools.partial(scatter_kernel, blocks),
        grid=(DEVICES // blocks,),
        in_specs=[pl.BlockSpec((blocks, ROWS, SLOTS), lambda i: (i, 0, 0))],
        out_specs=[pl.BlockSpec(shape, lambda i: (0, 0, 0)) for shape in shapes],
        out_shape=[jax.ShapeDtypeStruct(shape, BF16) for shape in shapes],
        scratch_shapes=[pltpu.VMEM((2 * rows, PLANE), F32)],
        compiler_params=params(),
        cost_estimate=cost(256 * PLANE * DEVICES * SLOTS, 4 * 2**20),
    )(arrived)


def gather_kernel(blocks, in_ref, grid_ref, out_ref):
    lines = 4
    placed = [places(in_ref[j].astype(F32)) for j in range(blocks)]
    total = None
    for y in range(0, CYD, lines):
        weights = jnp.concatenate(
            [plane_weights(pos_y, weight_z, y, lines) for _, pos_y, weight_z in placed], axis=1
        )
        product = jnp.dot(
            grid_ref[:, y * GZ : (y + lines) * GZ], weights, preferred_element_type=F32
        )
        total = product if total is None else total + product
    for j in range(blocks):
        for field in range(2):
            summed = None
            for x in range(CXD):
                row = (field * CXD + x) * CHANNELS
                part = total[row : row + CHANNELS, j * SLOTS : (j + 1) * SLOTS]
                part = part * hat(placed[j][0], float(x))
                summed = part if summed is None else summed + part
            out_ref[j, field * CHANNELS : (field + 1) * CHANNELS, :] = summed.astype(BF16)


def gather(arrived, grids):
    blocks = 16
    return pl.pallas_call(
        functools.partial(gather_kernel, blocks),
        grid=(DEVICES // blocks,),
        in_specs=[
            pl.BlockSpec((blocks, 8, SLOTS), lambda i: (i, 8, 0)),
            pl.BlockSpec((2 * CXD * CHANNELS, PLANE), lambda i: (0, 0)),
        ],
        out_specs=pl.BlockSpec((blocks, 2 * CHANNELS, SLOTS), lambda i: (i, 0, 0)),
        out_shape=jax.ShapeDtypeStruct((DEVICES, ROWS, SLOTS), BF16),
        compiler_params=params(),
        cost_estimate=cost(256 * PLANE * DEVICES * SLOTS, 4 * 2**20),
    )(arrived, grids)


def attach_kernel(parts_ref, held_ref, out_ref):
    del held_ref
    total = jnp.sum(parts_ref[...], axis=0)
    high = total.astype(BF16).astype(F32)
    both = jnp.concatenate([high, total - high], axis=0).astype(BF16)
    out_ref[...] = jnp.broadcast_to(both[None], out_ref.shape)


def attach(parts, payload):
    return pl.pallas_call(
        attach_kernel,
        grid=(1,),
        in_specs=[
            pl.BlockSpec((DEVICES, 4, SLOTS), lambda i: (0, 0, 0)),
            pl.BlockSpec(memory_space=pl.ANY),
        ],
        out_specs=pl.BlockSpec((DEVICES, 8, SLOTS), lambda i: (0, 8, 0)),
        out_shape=jax.ShapeDtypeStruct((DEVICES, ROWS, SLOTS), BF16),
        input_output_aliases={1: 0},
        compiler_params=params(),
        cost_estimate=cost(10**5, 2**19),
    )(parts, payload)


def halo(head_x, tail_x, head_y, tail_y, hh, ht, th, tt):
    count_a = lax.axis_size("aa")
    count_b = lax.axis_size("ba")

    def moved(piece, step_a, step_b):
        pairs = []
        for a in range(count_a):
            for b in range(count_b):
                to_a, to_b = a + step_a, b + step_b
                if 0 <= to_a < count_a and 0 <= to_b < count_b:
                    pairs.append((a * count_b + b, to_a * count_b + to_b))
        return lax.ppermute(piece, ("aa", "ba"), pairs)

    return (
        moved(tail_x, 0, 1),
        moved(head_x, 0, -1),
        moved(tail_y, 1, 0),
        moved(head_y, -1, 0),
        moved(tt, 1, 1),
        moved(th, -1, 1),
        moved(ht, 1, -1),
        moved(hh, -1, -1),
    )


def conv_kernel(
    own, x_low, x_high, y_low, y_high, ll, lh, hl, hh, w_one, w_back, w_two, w_last,
    out_ref, grads_ref, z0, z1, b0, b1, a0, a1, p0, p1, reduced,
):
    wide = PLANE + 4 * GZ
    mid = PLANE + 2 * GZ
    spot_a = lax.axis_index("aa")
    spot_b = lax.axis_index("ba")

    def shifted(value, even, odd):
        rows, lanes = value.shape
        value = value.astype(F32)
        depth = lax.rem(lax.broadcasted_iota(jnp.int32, (1, lanes), 1), GZ)
        for number in range(3):
            if number == 0:
                part = jnp.where(depth == 0, 0.0, pltpu.roll(value, 1, 1))
            elif number == 1:
                part = value
            else:
                part = jnp.where(depth == GZ - 1, 0.0, pltpu.roll(value, lanes - 1, 1))
            even[number * rows : (number + 1) * rows, :] = part.astype(BF16)
            turned = pltpu.roll(part, lanes - GZ, 1)
            odd[number * rows : (number + 1) * rows, :] = turned[:, : odd.shape[1]].astype(BF16)

    for field, (even, odd) in enumerate(((z0, z1), (b0, b1))):
        value = jnp.concatenate(
            [
                jnp.concatenate([ll[field], x_low[field], lh[field]], axis=1),
                jnp.concatenate([y_low[field], own[field], y_high[field]], axis=1),
                jnp.concatenate([hl[field], x_high[field], hh[field]], axis=1),
            ],
            axis=0,
        )
        shifted(value, even, odd)

    def convolved(weights, even, odd, lanes):
        total = jnp.dot(weights[0], even[:, :lanes], preferred_element_type=F32)
        total = total + jnp.dot(weights[1], odd[:, :lanes], preferred_element_type=F32)
        return total + jnp.dot(
            weights[2], even[:, 2 * GZ : 2 * GZ + lanes], preferred_element_type=F32
        )

    pre_one = convolved(w_one, z0, z1, mid)
    act_back = convolved(w_back, b0, b1, mid)
    plane = lax.div(lax.broadcasted_iota(jnp.int32, (6 * CHANNELS, 1), 0), CHANNELS)
    line = lax.div(lax.broadcasted_iota(jnp.int32, (1, mid), 1), GZ)
    outside_x = ((plane == 0) & (spot_b == 0)) | (
        (plane == CXD + 1) & (spot_b == lax.axis_size("ba") - 1)
    )
    outside_y = ((line == 0) & (spot_a == 0)) | (
        (line == CYD + 1) & (spot_a == lax.axis_size("aa") - 1)
    )
    inside = jnp.where(outside_x, 0.0, 1.0) * jnp.where(outside_y, 0.0, 1.0)
    sigma = jax.nn.sigmoid(pre_one)
    shifted((pre_one * sigma * inside).astype(BF16), a0, a1)
    slope = sigma * (1.0 + pre_one * (1.0 - sigma))
    shifted((act_back * slope * inside).astype(BF16), p0, p1)
    rows = 6 * CHANNELS
    first = rows + CHANNELS
    own_rows = CXD * CHANNELS
    grid_one = own[0].astype(F32) + convolved(w_two, a0, a1, PLANE)
    out_ref[:own_rows] = grid_one.astype(BF16)
    back_zero = own[1].astype(F32) + convolved(w_last, p0, p1, PLANE)
    out_ref[own_rows:] = back_zero.astype(BF16)

    upstream = (p1[first : first + own_rows, :], own[1])
    row_plane = lax.div(lax.broadcasted_iota(jnp.int32, (own_rows, rows), 0), CHANNELS)
    col_plane = lax.div(lax.broadcasted_iota(jnp.int32, (own_rows, rows), 1), CHANNELS)
    for conv in range(2):
        for step_y in range(3):
            for step_z in range(3):
                if conv == 0:
                    start = step_z * 8 * CHANNELS + CHANNELS
                    if step_y == 1:
                        field = z0[start : start + rows, 2 * GZ : 2 * GZ + PLANE]
                    else:
                        field = z1[start : start + rows, step_y * GZ : step_y * GZ + PLANE]
                else:
                    start = step_z * rows
                    if step_y == 1:
                        field = a1[start : start + rows, :]
                    else:
                        field = a0[start : start + rows, step_y * GZ : step_y * GZ + PLANE]
                product = lax.dot_general(upstream[conv], field, NT, preferred_element_type=F32)
                for step_x in range(3):
                    kept = jnp.where(col_plane == row_plane + step_x, product, 0.0)
                    folded = kept[:CHANNELS]
                    for x in range(1, CXD):
                        folded = folded + kept[x * CHANNELS : (x + 1) * CHANNELS]
                    at = (conv * 27 + step_x * 9 + step_y * 3 + step_z) * CHANNELS
                    reduced[at : at + CHANNELS, :] = folded
    quarter = 2 * 27 * CHANNELS // 4
    total = None
    for part in range(4):
        source = lax.broadcasted_iota(jnp.int32, (rows, 128), 0)
        target = lax.broadcasted_iota(jnp.int32, (rows, 128), 1)
        chosen = (target == lax.rem(source, CHANNELS) + part * CHANNELS).astype(F32)
        product = jnp.dot(
            reduced[part * quarter : (part + 1) * quarter, :],
            chosen,
            preferred_element_type=F32,
            precision=lax.Precision.HIGHEST,
        )
        total = product if total is None else total + product
    grads_ref[...] = total


def band(kernel, planes):
    taps = kernel.reshape(3, 3, 3, CHANNELS, CHANNELS)
    taps = jnp.transpose(taps, (1, 3, 2, 0, 4))
    taps = jnp.pad(taps, ((0, 0), (0, 0), (0, 0), (0, planes - 1), (0, 0)))
    return taps.reshape(3, CHANNELS, 3 * (planes + 2) * CHANNELS)


def toeplitz_kernel(*refs):
    for band_ref, out_ref in zip(refs[:4], refs[4:]):
        for step in range(3):
            first = band_ref[step].astype(F32)
            for x in range(out_ref.shape[1] // CHANNELS):
                moved = first if x == 0 else pltpu.roll(first, x * CHANNELS, 1)
                out_ref[step, x * CHANNELS : (x + 1) * CHANNELS, :] = moved.astype(BF16)


def toeplitz(kernel_one, kernel_two):
    bands = (
        band(kernel_one, 6),
        band(flipped(kernel_two), 6),
        band(kernel_two, 4),
        band(flipped(kernel_one), 4),
    )
    return pl.pallas_call(
        toeplitz_kernel,
        out_shape=[
            jax.ShapeDtypeStruct((3, planes * CHANNELS, 3 * (planes + 2) * CHANNELS), BF16)
            for planes in (6, 6, 4, 4)
        ],
        compiler_params=params(),
        cost_estimate=cost(10**7, 4 * 2**20),
    )(*bands)


def conv_block(grids, edges, weights):
    wide = PLANE + 4 * GZ
    mid = PLANE + 2 * GZ
    rows_one = 3 * 8 * CHANNELS
    rows_two = 3 * 6 * CHANNELS
    quarter = 2 * 27 * CHANNELS // 4
    return pl.pallas_call(
        conv_kernel,
        out_shape=(
            jax.ShapeDtypeStruct((2 * CXD * CHANNELS, PLANE), BF16),
            jax.ShapeDtypeStruct((quarter, 128), F32),
        ),
        scratch_shapes=[
            pltpu.VMEM((rows_one, wide), BF16),
            pltpu.VMEM((rows_one, wide), BF16),
            pltpu.VMEM((rows_one, wide), BF16),
            pltpu.VMEM((rows_one, wide), BF16),
            pltpu.VMEM((rows_two, mid), BF16),
            pltpu.VMEM((rows_two, PLANE), BF16),
            pltpu.VMEM((rows_two, mid), BF16),
            pltpu.VMEM((rows_two, PLANE), BF16),
            pltpu.VMEM((2 * 27 * CHANNELS, 6 * CHANNELS), F32),
        ],
        compiler_params=params(),
        cost_estimate=cost(6 * 10**9, 8 * 2**20),
    )(grids, *edges, *weights)


def unroute_kernel(
    ret_ref, slot_ref, owner_ref, local_ref, back_ref,
    out_ref, grad_ref, kernels_ref, in_ref, mlp_ref, table,
):
    rows = 2 * CHANNELS
    for high in range(HIGH):
        for low in range(LOW):
            table[low * rows : (low + 1) * rows, high * SLOTS : (high + 1) * SLOTS] = ret_ref[
                high * LOW + low, :rows, :
            ]
    width = 512
    for step in range(PARTICLES // width):
        lanes = slice(step * width, (step + 1) * width)
        slot_ids = lax.broadcasted_iota(jnp.int32, (HIGH * SLOTS, width), 0)
        hot = (slot_ids == slot_ref[:, lanes]).astype(F32).astype(BF16)
        found = jnp.dot(table[...], hot, preferred_element_type=F32)
        low = lax.rem(owner_ref[:, lanes], LOW)
        mine = None
        for group in range(LOW):
            part = jnp.where(low == group, found[group * rows : (group + 1) * rows], 0.0)
            mine = part if mine is None else mine + part
        out_ref[:, lanes] = (mine[:CHANNELS] + local_ref[:, lanes]).astype(BF16)
        grad_ref[:, lanes] = (mine[CHANNELS:] + back_ref[:, lanes]).astype(BF16)

    halves = ret_ref[:, rows:, :].astype(F32)
    summed = (halves + pltpu.roll(halves, 4, 1)).reshape(DEVICES // 2, 2, 8, SLOTS)
    upper = lax.broadcasted_iota(jnp.int32, (DEVICES // 2, 8, SLOTS), 1) < 4
    summed = jnp.where(upper, summed[:, 0], summed[:, 1]).reshape(4 * DEVICES, SLOTS)
    quarter = 2 * 27 * CHANNELS // 4
    for part in range(4):
        moved = summed[:quarter]
        if part:
            moved = pltpu.roll(moved, 128 - part * CHANNELS, 1)
        kernels_ref[part * quarter : (part + 1) * quarter, :] = moved[:, :CHANNELS]
    both = summed[quarter : quarter + 2 * CHANNELS]
    in_ref[...] = jnp.concatenate([both, both], axis=0).T[:, :CHANNELS]
    mlp_ref[...] = both[CHANNELS:]


def unroute(returned, slot, owner, local_out, local_back):
    shape = jax.ShapeDtypeStruct((CHANNELS, PARTICLES), BF16)
    return pl.pallas_call(
        unroute_kernel,
        out_shape=(
            shape,
            shape,
            jax.ShapeDtypeStruct((2 * 27 * CHANNELS, CHANNELS), F32),
            jax.ShapeDtypeStruct((128, CHANNELS), F32),
            jax.ShapeDtypeStruct((CHANNELS, 128), F32),
        ),
        scratch_shapes=[pltpu.VMEM((LOW * 2 * CHANNELS, HIGH * SLOTS), BF16)],
        compiler_params=params(),
        cost_estimate=cost(1024 * 1024 * PARTICLES, 4 * 2**20),
    )(returned, slot, owner, local_out, local_back)


def exchanged(blocks):
    return lax.all_to_all(blocks, ("aa", "ba"), split_axis=0, concat_axis=0, tiled=True)


def local(features, cotangent, owner, offset, kernel_one, kernel_two, mlp_in, mlp_out):
    owner = owner.reshape(1, PARTICLES)
    payload = jnp.concatenate(
        [features, cotangent, offset, jnp.zeros((GROUP - 67, PARTICLES), BF16)], axis=0
    )
    outgoing, slot = route(owner, payload)
    arrived = exchanged(outgoing)
    local_out, local_back, small = network(features, cotangent, mlp_in, mlp_out)
    weights = toeplitz(kernel_one, kernel_two)
    arrived, weights, small = lax.optimization_barrier((arrived, weights, small))
    grids, *edges = scatter(arrived)
    both_grids, grads = conv_block(grids, halo(*edges), weights)
    filler = jnp.zeros((4 * DEVICES - grads.shape[0] - small.shape[0], SLOTS), F32)
    parts = jnp.concatenate([grads, small, filler], axis=0).reshape(DEVICES, 4, SLOTS)
    payload = attach(exchanged(parts), gather(arrived, both_grids))
    returned = exchanged(payload)
    particle_out, feat_grad, grad_kernels, grad_in, grad_out = unroute(
        returned, slot, owner, local_out, local_back
    )
    grad_kernels = grad_kernels.reshape(2, 27, CHANNELS, CHANNELS)
    return particle_out, feat_grad, grad_kernels, grad_in, grad_out


def solution(mesh):
    in_specs = (
        P(None, ("aa", "ba")),
        P(None, ("aa", "ba")),
        P(("aa", "ba"), None),
        P(None, ("aa", "ba")),
        P(),
        P(),
        P(),
        P(),
    )
    out_specs = (P(None, ("aa", "ba")), P(None, ("aa", "ba")), P(), P(), P())
    return jax.shard_map(local, mesh=mesh, in_specs=in_specs, out_specs=out_specs, check_vma=False)
```

```python
import functools

import jax
import jax.numpy as jnp
from jax import lax
from jax.experimental import pallas as pl
from jax.experimental.pallas import tpu as pltpu
from jax.sharding import PartitionSpec as P

F32 = jnp.float32
BF16 = jnp.bfloat16
NT = (((1,), (1,)), ((), ()))

DEVICES = 128
SLOTS = 128
PARTICLES = 4096
CHANNELS = 32
GZ = 64
CXD = 4
CYD = 32
PLANE = CYD * GZ
ROWS = 72
HALF = 40
TILE = 2 * GZ
TILES = PLANE // TILE
WIDE = PLANE + 4 * TILE
MID = PLANE + 2 * TILE
LOW = 16
HIGH = DEVICES // LOW
VMEM_LIMIT = 56 * 2**20


def params():
    return pltpu.CompilerParams(vmem_limit_bytes=VMEM_LIMIT)


def cost(macs, moved):
    return pl.CostEstimate(flops=2 * macs, bytes_accessed=moved, transcendentals=0)


def rows16(row):
    return jnp.broadcast_to(row, (16, row.shape[1]))


def silu_slope(value):
    sigma_value = jax.nn.sigmoid(value)
    return sigma_value * (1.0 + value * (1.0 - sigma_value))


def flipped(kernel):
    return jnp.transpose(kernel[::-1], (0, 2, 1))


def route_kernel(owner_ref, feat_ref, cot_ref, off_ref, out_ref, slot_ref, spread):
    block = 256
    owner_ids = lax.broadcasted_iota(jnp.int32, (DEVICES, block), 0)
    before = lax.broadcasted_iota(jnp.int32, (block, block + 128), 0)
    after = lax.broadcasted_iota(jnp.int32, (block, block + 128), 1)
    prefix = ((before < after) | (after >= block)).astype(F32).astype(BF16)
    base = jnp.zeros((DEVICES, 128), F32)
    ranks = []
    for number in range(PARTICLES // block):
        hot = (owner_ids == owner_ref[:, number * block : (number + 1) * block]).astype(F32)
        counted = jnp.dot(hot.astype(BF16), prefix, preferred_element_type=F32)
        earlier = counted[:, :block] + jnp.concatenate([base, base], axis=1)
        ranks.append(jnp.sum(hot * earlier, axis=0, keepdims=True))
        base = base + counted[:, block:]
    rank = jnp.concatenate(ranks, axis=1).astype(jnp.int32)
    owner = owner_ref[...]
    low = lax.rem(owner, LOW)
    slot = lax.div(owner, LOW) * SLOTS + rank
    slot_ref[...] = slot
    for group in range(LOW):
        mask = rows16((low == group).astype(F32)).astype(BF16)
        for field, source in enumerate((feat_ref, cot_ref)):
            for part in range(0, CHANNELS, 16):
                at = group * 2 * CHANNELS + field * CHANNELS + part
                spread[at : at + 16, :] = source[part : part + 16, :] * mask
    tail = LOW * 2 * CHANNELS
    offset = off_ref[...].astype(F32)
    nothing = jnp.zeros((1, PARTICLES), F32)
    offset = jnp.concatenate([offset, nothing, offset, nothing], axis=0)
    line = lax.div(lax.broadcasted_iota(jnp.int32, (8, PARTICLES), 0), 4)
    for group in range(0, LOW, 4):
        parts = [jnp.where(low == group + pair + line, offset, 0.0) for pair in (0, 2)]
        spread[tail + group * 4 : tail + group * 4 + 16, :] = jnp.concatenate(
            parts, axis=0
        ).astype(BF16)
    width = 256
    for step in range(HIGH * SLOTS // width):
        slot_ids = lax.broadcasted_iota(jnp.int32, (width, PARTICLES), 0) + step * width
        hot = (slot_ids == slot).astype(F32).astype(BF16)
        placed = lax.dot_general(spread[...], hot, NT, preferred_element_type=F32)
        for part in range(width // SLOTS):
            high = step * (width // SLOTS) + part
            lanes = slice(part * SLOTS, (part + 1) * SLOTS)
            for group in range(LOW):
                values = placed[group * 2 * CHANNELS : (group + 1) * 2 * CHANNELS, lanes]
                at = tail + group // 2 * 8
                where = placed[at : at + 8, lanes]
                if group % 2:
                    where = pltpu.roll(where, 4, 0)
                out_ref[high * LOW + group] = jnp.concatenate([values, where], axis=0).astype(BF16)


def route(owner, features, cotangent, offset):
    rows = LOW * (2 * CHANNELS + 4)
    return pl.pallas_call(
        route_kernel,
        out_shape=(
            jax.ShapeDtypeStruct((DEVICES, ROWS, SLOTS), BF16),
            jax.ShapeDtypeStruct((1, PARTICLES), jnp.int32),
        ),
        scratch_shapes=[pltpu.VMEM((rows, PARTICLES), BF16)],
        compiler_params=params(),
        cost_estimate=cost(rows * PARTICLES * HIGH * SLOTS, 3 * 2**20),
    )(owner, features, cotangent, offset)


def network_kernel(feat_ref, cot_ref, in_ref, out_ref, in_t_ref, out_t_ref, local_ref, back_ref, grads_ref):
    step = pl.program_id(0)
    features = feat_ref[...]
    cotangent = cot_ref[...]
    hidden_pre = jnp.dot(in_ref[...], features, preferred_element_type=F32)
    hidden = jax.nn.silu(hidden_pre).astype(BF16)
    local_ref[...] = jnp.dot(out_ref[...], hidden, preferred_element_type=F32)
    hidden_back = jnp.dot(out_t_ref[...], cotangent, preferred_element_type=F32)
    pre_grad = (hidden_back * silu_slope(hidden_pre)).astype(BF16)
    back_ref[...] = jnp.dot(in_t_ref[...], pre_grad, preferred_element_type=F32)
    grad_in = lax.dot_general(features, pre_grad, NT, preferred_element_type=F32)
    grad_out = lax.dot_general(cotangent, hidden, NT, preferred_element_type=F32)
    both = jnp.concatenate([grad_in, grad_out], axis=0)

    @pl.when(step == 0)
    def first():
        grads_ref[...] = both

    @pl.when(step > 0)
    def later():
        grads_ref[...] += both


def network(features, cotangent, mlp_in, mlp_out):
    width = 1024
    hidden = mlp_in.shape[0]

    def whole(rows, columns):
        return pl.BlockSpec((rows, columns), lambda i: (0, 0))

    wide = pl.BlockSpec((CHANNELS, width), lambda i: (0, i))
    return pl.pallas_call(
        network_kernel,
        grid=(PARTICLES // width,),
        in_specs=[
            wide,
            wide,
            whole(hidden, CHANNELS),
            whole(CHANNELS, hidden),
            whole(CHANNELS, hidden),
            whole(hidden, CHANNELS),
        ],
        out_specs=(wide, wide, whole(2 * CHANNELS, hidden)),
        out_shape=(
            jax.ShapeDtypeStruct((CHANNELS, PARTICLES), F32),
            jax.ShapeDtypeStruct((CHANNELS, PARTICLES), F32),
            jax.ShapeDtypeStruct((2 * CHANNELS, hidden), F32),
        ),
        compiler_params=params(),
        cost_estimate=cost(6 * 128 * 128 * PARTICLES, 2 * 2**20),
    )(features, cotangent, mlp_in, mlp_out, mlp_in.T, mlp_out.T)


def hat(position, at):
    return jnp.maximum(1.0 - jnp.abs(position - at), 0.0)


def places(offset):
    pos_x = offset[0:1] * float(CXD - 1)
    pos_y = jnp.broadcast_to(offset[1:2] * float(CYD - 1), (8, SLOTS))
    pos_z = offset[2:3] * float(GZ - 1)
    depth = lax.broadcasted_iota(jnp.int32, (GZ, SLOTS), 0).astype(F32)
    return pos_x, pos_y, hat(pos_z, depth)


def plane_weights(pos_y, weight_z, first, count):
    rows = []
    for y in [tile + half * TILES for tile in range(first, first + count) for half in range(2)]:
        weight_y = hat(pos_y, float(y))
        for part in range(GZ // 8):
            rows.append(weight_y * weight_z[part * 8 : part * 8 + 8])
    return jnp.concatenate(rows, axis=0).astype(BF16)


def scatter_kernel(blocks, in_ref, out_ref, head_y, tail_y, total):
    step = pl.program_id(0)
    tiles = 2
    sources, placed = [], []
    for j in range(blocks):
        pos_x, pos_y, weight_z = places(in_ref[j, 64:72, :].astype(F32))
        placed.append((pos_y, weight_z))
        parts = []
        for field in range(2):
            values = in_ref[j, field * CHANNELS : (field + 1) * CHANNELS, :].astype(F32)
            for x in range(CXD):
                parts.append((values * hat(pos_x, float(x))).astype(BF16))
        sources.append(jnp.concatenate(parts, axis=0))
    source = jnp.concatenate(sources, axis=1)

    @pl.when(step == 0)
    def first():
        total[...] = jnp.zeros_like(total)

    for tile in range(0, TILES, tiles):
        weights = jnp.concatenate([plane_weights(*place, tile, tiles) for place in placed], axis=1)
        total[:, tile * TILE : (tile + tiles) * TILE] += lax.dot_general(
            source, weights, NT, preferred_element_type=F32
        )

    @pl.when(step == pl.num_programs(0) - 1)
    def last():
        rows = CXD * CHANNELS
        for field in range(2):
            cells = total[field * rows : (field + 1) * rows].astype(BF16)
            out_ref[field] = cells
            head_y[field] = cells[:, : 2 * TILE]
            tail_y[field] = cells[:, PLANE - 2 * TILE :]


def scatter(arrived):
    blocks = 16
    rows = CXD * CHANNELS
    shapes = [(2, rows, PLANE), (2, rows, 2 * TILE), (2, rows, 2 * TILE)]
    return pl.pallas_call(
        functools.partial(scatter_kernel, blocks),
        grid=(DEVICES // blocks,),
        in_specs=[pl.BlockSpec((blocks, ROWS, SLOTS), lambda i: (i, 0, 0))],
        out_specs=[pl.BlockSpec(shape, lambda i: (0, 0, 0)) for shape in shapes],
        out_shape=[jax.ShapeDtypeStruct(shape, BF16) for shape in shapes],
        scratch_shapes=[pltpu.VMEM((2 * rows, PLANE), F32)],
        compiler_params=params(),
        cost_estimate=cost(256 * PLANE * DEVICES * SLOTS, 4 * 2**20),
    )(arrived)


def gather_kernel(blocks, *refs):
    in_ref, grid_ref, out_ref = refs[0], refs[1], refs[-1]
    tiles = 2
    placed = [places(in_ref[j].astype(F32)) for j in range(blocks)]
    total = None
    for tile in range(0, TILES, tiles):
        weights = jnp.concatenate(
            [plane_weights(pos_y, weight_z, tile, tiles) for _, pos_y, weight_z in placed], axis=1
        )
        product = jnp.dot(
            grid_ref[:, tile * TILE : (tile + tiles) * TILE], weights, preferred_element_type=F32
        )
        total = product if total is None else total + product
    for j in range(blocks):
        summed = None
        for x in range(CXD):
            part = total[x * CHANNELS : (x + 1) * CHANNELS, j * SLOTS : (j + 1) * SLOTS]
            part = part * hat(placed[j][0], float(x))
            summed = part if summed is None else summed + part
        if len(refs) == 3:
            out_ref[j, :CHANNELS, :] = summed.astype(BF16)
        else:
            sums = refs[2][j // 2]
            high = sums.astype(BF16).astype(F32)
            rest = sums - high
            upper = lax.broadcasted_iota(jnp.int32, (8, SLOTS), 0) < 4
            if j % 2:
                both = jnp.where(upper, pltpu.roll(high, 4, 0), rest)
            else:
                both = jnp.where(upper, high, pltpu.roll(rest, 4, 0))
            out_ref[j] = jnp.concatenate([summed, both], axis=0).astype(BF16)


def gather(arrived, grids, *parts):
    blocks = 16
    rows = HALF if parts else CHANNELS
    return pl.pallas_call(
        functools.partial(gather_kernel, blocks),
        grid=(DEVICES // blocks,),
        in_specs=[
            pl.BlockSpec((blocks, 8, SLOTS), lambda i: (i, 8, 0)),
            pl.BlockSpec((CXD * CHANNELS, PLANE), lambda i: (0, 0)),
        ]
        + [pl.BlockSpec((blocks // 2, 8, SLOTS), lambda i: (i, 0, 0)) for _ in parts],
        out_specs=pl.BlockSpec((blocks, rows, SLOTS), lambda i: (i, 0, 0)),
        out_shape=jax.ShapeDtypeStruct((DEVICES, HALF, SLOTS), BF16),
        compiler_params=params(),
        cost_estimate=cost(128 * PLANE * DEVICES * SLOTS, 3 * 2**20),
    )(arrived, grids, *parts)


def attach_kernel(parts_ref, held_ref, out_ref):
    del held_ref
    total = jnp.sum(parts_ref[...].astype(F32), axis=0)
    total = total + pltpu.roll(total, 4, 0)
    high = total.astype(BF16).astype(F32)
    upper = lax.broadcasted_iota(jnp.int32, (8, SLOTS), 0) < 4
    both = jnp.where(upper, high, total - high).astype(BF16)
    out_ref[...] = jnp.broadcast_to(both[None], out_ref.shape)


def attach(returned, payload):
    rows = pl.BlockSpec((DEVICES, 8, SLOTS), lambda i: (0, CHANNELS // 8, 0))
    return pl.pallas_call(
        attach_kernel,
        grid=(1,),
        in_specs=[rows, pl.BlockSpec(memory_space=pl.ANY)],
        out_specs=rows,
        out_shape=jax.ShapeDtypeStruct((DEVICES, HALF, SLOTS), BF16),
        input_output_aliases={1: 0},
        compiler_params=params(),
        cost_estimate=cost(10**5, 2**19),
    )(returned, payload)


def moved(piece, axis, step):
    count = lax.axis_size(axis)
    pairs = [(i, i + step) for i in range(count) if 0 <= i + step < count]
    return lax.ppermute(piece, axis, pairs)


def extend_kernel(own, low, high, out_ref, head_x, tail_x):
    half = lax.rem(lax.div(lax.broadcasted_iota(jnp.int32, (1, 2 * TILE), 1), GZ), 2)
    rows = CXD * CHANNELS
    for field in range(2):
        first = own[field, :, : 2 * TILE].astype(F32)
        last = own[field, :, PLANE - 2 * TILE :].astype(F32)
        below = jnp.where(half == 1, low[field].astype(F32), last)
        above = jnp.where(half == 0, high[field].astype(F32), first)
        sides = []
        for side in (below, above):
            turned = [pltpu.roll(side[:, at : at + TILE], GZ, 1) for at in (0, TILE)]
            sides.append(jnp.concatenate(turned, axis=1).astype(BF16))
        cells = jnp.concatenate([sides[0], own[field], sides[1]], axis=1)
        out_ref[field] = cells
        head_x[field] = cells[: rows // 2]
        tail_x[field] = cells[rows // 2 :]


def extend(grids, low, high):
    rows = CXD * CHANNELS
    return pl.pallas_call(
        extend_kernel,
        out_shape=[
            jax.ShapeDtypeStruct((2, count, WIDE), BF16) for count in (rows, rows // 2, rows // 2)
        ],
        compiler_params=params(),
        cost_estimate=cost(10**6, 5 * 2**20),
    )(grids, low, high)


def conv_kernel(
    own, x_low, x_high, w_one, w_back, w_two, w_last, small_ref,
    out_ref, back_ref, grads_ref, zeros, backs, acts, pres, reduced,
):
    spot_a = lax.axis_index("aa")
    spot_b = lax.axis_index("ba")

    def shifted(value, out):
        rows, lanes = value.shape
        depth = lax.rem(lax.broadcasted_iota(jnp.int32, (1, lanes), 1), GZ)
        wide = value.astype(F32)
        before = jnp.where(depth == 0, 0.0, pltpu.roll(wide, 1, 1))
        after = jnp.where(depth == GZ - 1, 0.0, pltpu.roll(wide, lanes - 1, 1))
        out[:rows, :] = before.astype(BF16)
        out[rows : 2 * rows, :] = value
        out[2 * rows :, :] = after.astype(BF16)

    for field, out in enumerate((zeros, backs)):
        shifted(jnp.concatenate([x_low[field], own[field], x_high[field]], axis=0), out)

    def convolved(weights, source, lanes):
        total = None
        for step in range(3):
            product = jnp.dot(
                weights[step],
                source[:, step * TILE : step * TILE + lanes],
                preferred_element_type=F32,
            )
            total = product if total is None else total + product
        return total

    pre_one = convolved(w_one, zeros, MID)
    act_back = convolved(w_back, backs, MID)
    plane = lax.div(lax.broadcasted_iota(jnp.int32, (6 * CHANNELS, 1), 0), CHANNELS)
    line = lax.div(lax.broadcasted_iota(jnp.int32, (1, MID), 1), GZ)
    outside_x = ((plane == 0) & (spot_b == 0)) | (
        (plane == CXD + 1) & (spot_b == lax.axis_size("ba") - 1)
    )
    outside_y = ((line == 0) & (spot_a == 0)) | (
        (line == MID // GZ - 1) & (spot_a == lax.axis_size("aa") - 1)
    )
    inside = jnp.where(outside_x, 0.0, 1.0) * jnp.where(outside_y, 0.0, 1.0)
    sigma = jax.nn.sigmoid(pre_one)
    shifted((pre_one * sigma * inside).astype(BF16), acts)
    slope = sigma * (1.0 + pre_one * (1.0 - sigma))
    shifted((act_back * slope * inside).astype(BF16), pres)
    rows = 6 * CHANNELS
    first = rows + CHANNELS
    own_rows = CXD * CHANNELS
    inner = slice(2 * TILE, 2 * TILE + PLANE)
    grid_one = own[0, :, inner].astype(F32) + convolved(w_two, acts, PLANE)
    out_ref[...] = grid_one.astype(BF16)
    back_zero = own[1, :, inner].astype(F32) + convolved(w_last, pres, PLANE)
    back_ref[...] = back_zero.astype(BF16)

    upstream = (pres[first : first + own_rows, TILE : TILE + PLANE], own[1, :, inner])
    row_plane = lax.div(lax.broadcasted_iota(jnp.int32, (own_rows, rows), 0), CHANNELS)
    col_plane = lax.div(lax.broadcasted_iota(jnp.int32, (own_rows, rows), 1), CHANNELS)
    for conv in range(2):
        for step_y in range(3):
            for step_z in range(3):
                if conv == 0:
                    start = step_z * 8 * CHANNELS + CHANNELS
                    at = (step_y + 1) * TILE
                    field = zeros[start : start + rows, at : at + PLANE]
                else:
                    at = step_y * TILE
                    field = acts[step_z * rows : (step_z + 1) * rows, at : at + PLANE]
                product = lax.dot_general(upstream[conv], field, NT, preferred_element_type=F32)
                for step_x in range(3):
                    kept = jnp.where(col_plane == row_plane + step_x, product, 0.0)
                    folded = kept[:CHANNELS]
                    for x in range(1, CXD):
                        folded = folded + kept[x * CHANNELS : (x + 1) * CHANNELS]
                    at = (conv * 27 + step_x * 9 + step_y * 3 + step_z) * CHANNELS
                    reduced[at : at + CHANNELS, :] = folded
    quarter = 2 * 27 * CHANNELS // 4
    total = None
    for part in range(4):
        source = lax.broadcasted_iota(jnp.int32, (rows, 128), 0)
        target = lax.broadcasted_iota(jnp.int32, (rows, 128), 1)
        chosen = (target == lax.rem(source, CHANNELS) + part * CHANNELS).astype(F32)
        product = jnp.dot(
            reduced[part * quarter : (part + 1) * quarter, :],
            chosen,
            preferred_element_type=F32,
            precision=lax.Precision.HIGHEST,
        )
        total = product if total is None else total + product
    small = small_ref[...]
    filler = jnp.zeros((4 * DEVICES - quarter - small.shape[0], SLOTS), F32)
    grads_ref[:quarter] = total
    grads_ref[quarter:] = jnp.concatenate([small, filler], axis=0)


def band(kernel, planes):
    taps = kernel.reshape(3, 3, 3, CHANNELS, CHANNELS)
    taps = jnp.transpose(taps, (1, 3, 2, 0, 4))
    taps = jnp.pad(taps, ((0, 0), (0, 0), (0, 0), (0, planes - 1), (0, 0)))
    return taps.reshape(3, CHANNELS, 3 * (planes + 2) * CHANNELS)


def toeplitz_kernel(*refs):
    for band_ref, out_ref in zip(refs[:4], refs[4:]):
        for step in range(3):
            first = band_ref[step].astype(F32)
            for x in range(out_ref.shape[1] // CHANNELS):
                moved = first if x == 0 else pltpu.roll(first, x * CHANNELS, 1)
                out_ref[step, x * CHANNELS : (x + 1) * CHANNELS, :] = moved.astype(BF16)


def toeplitz(kernel_one, kernel_two):
    bands = (
        band(kernel_one, 6),
        band(flipped(kernel_two), 6),
        band(kernel_two, 4),
        band(flipped(kernel_one), 4),
    )
    return pl.pallas_call(
        toeplitz_kernel,
        out_shape=[
            jax.ShapeDtypeStruct((3, planes * CHANNELS, 3 * (planes + 2) * CHANNELS), BF16)
            for planes in (6, 6, 4, 4)
        ],
        compiler_params=params(),
        cost_estimate=cost(10**7, 4 * 2**20),
    )(*bands)


def conv_block(grids, low, high, weights, small):
    rows_one = 3 * 8 * CHANNELS
    rows_two = 3 * 6 * CHANNELS
    shape = jax.ShapeDtypeStruct((CXD * CHANNELS, PLANE), BF16)
    return pl.pallas_call(
        conv_kernel,
        out_shape=(shape, shape, jax.ShapeDtypeStruct((4 * DEVICES, SLOTS), F32)),
        scratch_shapes=[
            pltpu.VMEM((rows_one, WIDE), BF16),
            pltpu.VMEM((rows_one, WIDE), BF16),
            pltpu.VMEM((rows_two, MID), BF16),
            pltpu.VMEM((rows_two, MID), BF16),
            pltpu.VMEM((2 * 27 * CHANNELS, 6 * CHANNELS), F32),
        ],
        compiler_params=params(),
        cost_estimate=cost(6 * 10**9, 8 * 2**20),
    )(grids, low, high, *weights, small)


def unroute_kernel(ret_ref, slot_ref, owner_ref, local_ref, out_ref, *refs):
    rows = CHANNELS
    table = refs[-1]
    for high in range(HIGH):
        for low in range(LOW):
            table[low * rows : (low + 1) * rows, high * SLOTS : (high + 1) * SLOTS] = ret_ref[
                high * LOW + low, :rows, :
            ]
    width = 512
    for step in range(PARTICLES // width):
        lanes = slice(step * width, (step + 1) * width)
        slot_ids = lax.broadcasted_iota(jnp.int32, (HIGH * SLOTS, width), 0)
        hot = (slot_ids == slot_ref[:, lanes]).astype(F32).astype(BF16)
        found = jnp.dot(table[...], hot, preferred_element_type=F32)
        low = lax.rem(owner_ref[:, lanes], LOW)
        mine = None
        for group in range(LOW):
            part = jnp.where(low == group, found[group * rows : (group + 1) * rows], 0.0)
            mine = part if mine is None else mine + part
        out_ref[:, lanes] = (mine + local_ref[:, lanes]).astype(BF16)
    if len(refs) == 1:
        return

    kernels_ref, in_ref, mlp_ref = refs[:3]
    halves = ret_ref[:, rows:, :].astype(F32)
    summed = (halves + pltpu.roll(halves, 4, 1)).reshape(DEVICES // 2, 2, 8, SLOTS)
    upper = lax.broadcasted_iota(jnp.int32, (DEVICES // 2, 8, SLOTS), 1) < 4
    summed = jnp.where(upper, summed[:, 0], summed[:, 1]).reshape(4 * DEVICES, SLOTS)
    quarter = 2 * 27 * CHANNELS // 4
    for part in range(4):
        turned = summed[:quarter]
        if part:
            turned = pltpu.roll(turned, 128 - part * CHANNELS, 1)
        kernels_ref[part * quarter : (part + 1) * quarter, :] = turned[:, :CHANNELS]
    in_ref[...] = summed[quarter : quarter + CHANNELS]
    mlp_ref[...] = summed[quarter + CHANNELS : quarter + 2 * CHANNELS]


def unroute(returned, slot, owner, addend, sums):
    shapes = [jax.ShapeDtypeStruct((CHANNELS, PARTICLES), BF16)]
    if sums:
        shapes += [
            jax.ShapeDtypeStruct((2 * 27 * CHANNELS, CHANNELS), F32),
            jax.ShapeDtypeStruct((CHANNELS, 128), F32),
            jax.ShapeDtypeStruct((CHANNELS, 128), F32),
        ]
    return pl.pallas_call(
        unroute_kernel,
        out_shape=shapes,
        scratch_shapes=[pltpu.VMEM((LOW * CHANNELS, HIGH * SLOTS), BF16)],
        compiler_params=params(),
        cost_estimate=cost(512 * 1024 * PARTICLES, 3 * 2**20),
    )(returned, slot, owner, addend)


def exchanged(blocks):
    return lax.all_to_all(blocks, ("aa", "ba"), split_axis=0, concat_axis=0, tiled=True)


def local(features, cotangent, owner, offset, kernel_one, kernel_two, mlp_in, mlp_out):
    owner = owner.reshape(1, PARTICLES)
    outgoing, slot = route(owner, features, cotangent, offset)
    arrived = exchanged(outgoing)
    local_out, local_back, small = network(features, cotangent, mlp_in, mlp_out)
    weights = toeplitz(kernel_one, kernel_two)
    arrived, weights, small = lax.optimization_barrier((arrived, weights, small))
    grids, head_y, tail_y = scatter(arrived)
    grids, head_x, tail_x = extend(grids, moved(tail_y, "aa", 1), moved(head_y, "aa", -1))
    grid_one, back_zero, parts = conv_block(
        grids, moved(tail_x, "ba", 1), moved(head_x, "ba", -1), weights, small
    )
    first = exchanged(gather(arrived, grid_one, parts.reshape(DEVICES // 2, 8, SLOTS)))
    second = exchanged(attach(first, gather(arrived, back_zero)))
    (particle_out,) = unroute(first, slot, owner, local_out, False)
    feat_grad, grad_kernels, grad_in, grad_out = unroute(second, slot, owner, local_back, True)
    grad_kernels = grad_kernels.reshape(2, 27, CHANNELS, CHANNELS)
    return particle_out, feat_grad, grad_kernels, grad_in.T, grad_out


def solution(mesh):
    in_specs = (
        P(None, ("aa", "ba")),
        P(None, ("aa", "ba")),
        P(("aa", "ba"), None),
        P(None, ("aa", "ba")),
        P(),
        P(),
        P(),
        P(),
    )
    out_specs = (P(None, ("aa", "ba")), P(None, ("aa", "ba")), P(), P(), P())
    return jax.shard_map(local, mesh=mesh, in_specs=in_specs, out_specs=out_specs, check_vma=False)
```

```python
import functools

import jax
import jax.numpy as jnp
from jax import lax
from jax.experimental import pallas as pl
from jax.experimental.pallas import tpu as pltpu
from jax.sharding import PartitionSpec as P

F32 = jnp.float32
BF16 = jnp.bfloat16
NT = (((1,), (1,)), ((), ()))

DEVICES = 128
SLOTS = 128
PARTICLES = 4096
CHANNELS = 32
GZ = 64
CXD = 4
CYD = 32
PLANE = CYD * GZ
ROWS = 72
HALF = 40
TILE = 2 * GZ
TILES = PLANE // TILE
WIDE = PLANE + 4 * TILE
MID = PLANE + 2 * TILE
LOW = 16
HIGH = DEVICES // LOW


def params(mebibytes):
    return pltpu.CompilerParams(vmem_limit_bytes=mebibytes * 2**20)


def cost(macs, moved):
    return pl.CostEstimate(flops=2 * macs, bytes_accessed=moved, transcendentals=0)


def rows16(row):
    return jnp.broadcast_to(row, (16, row.shape[1]))


def silu_slope(value):
    sigma_value = jax.nn.sigmoid(value)
    return sigma_value * (1.0 + value * (1.0 - sigma_value))


def flipped(kernel):
    return jnp.transpose(kernel[::-1], (0, 2, 1))


def route_kernel(owner_ref, feat_ref, cot_ref, off_ref, out_ref, slot_ref, spread):
    block = 256
    owner_ids = lax.broadcasted_iota(jnp.int32, (DEVICES, block), 0)
    before = lax.broadcasted_iota(jnp.int32, (block, block + 128), 0)
    after = lax.broadcasted_iota(jnp.int32, (block, block + 128), 1)
    prefix = ((before < after) | (after >= block)).astype(F32).astype(BF16)
    base = jnp.zeros((DEVICES, 128), F32)
    ranks = []
    for number in range(PARTICLES // block):
        hot = (owner_ids == owner_ref[:, number * block : (number + 1) * block]).astype(F32)
        counted = jnp.dot(hot.astype(BF16), prefix, preferred_element_type=F32)
        earlier = counted[:, :block] + jnp.concatenate([base, base], axis=1)
        ranks.append(jnp.sum(hot * earlier, axis=0, keepdims=True))
        base = base + counted[:, block:]
    rank = jnp.concatenate(ranks, axis=1).astype(jnp.int32)
    owner = owner_ref[...]
    low = lax.rem(owner, LOW)
    slot = lax.div(owner, LOW) * SLOTS + rank
    slot_ref[...] = slot
    for group in range(LOW):
        mask = rows16((low == group).astype(F32)).astype(BF16)
        for field, source in enumerate((feat_ref, cot_ref)):
            for part in range(0, CHANNELS, 16):
                at = group * 2 * CHANNELS + field * CHANNELS + part
                spread[at : at + 16, :] = source[part : part + 16, :] * mask
    tail = LOW * 2 * CHANNELS
    offset = off_ref[...].astype(F32)
    nothing = jnp.zeros((1, PARTICLES), F32)
    offset = jnp.concatenate([offset, nothing, offset, nothing], axis=0)
    line = lax.div(lax.broadcasted_iota(jnp.int32, (8, PARTICLES), 0), 4)
    for group in range(0, LOW, 4):
        parts = [jnp.where(low == group + pair + line, offset, 0.0) for pair in (0, 2)]
        spread[tail + group * 4 : tail + group * 4 + 16, :] = jnp.concatenate(
            parts, axis=0
        ).astype(BF16)
    width = 256
    for step in range(HIGH * SLOTS // width):
        slot_ids = lax.broadcasted_iota(jnp.int32, (width, PARTICLES), 0) + step * width
        hot = (slot_ids == slot).astype(F32).astype(BF16)
        placed = lax.dot_general(spread[...], hot, NT, preferred_element_type=F32)
        for part in range(width // SLOTS):
            high = step * (width // SLOTS) + part
            lanes = slice(part * SLOTS, (part + 1) * SLOTS)
            for group in range(LOW):
                values = placed[group * 2 * CHANNELS : (group + 1) * 2 * CHANNELS, lanes]
                at = tail + group // 2 * 8
                where = placed[at : at + 8, lanes]
                if group % 2:
                    where = pltpu.roll(where, 4, 0)
                out_ref[high * LOW + group] = jnp.concatenate([values, where], axis=0).astype(BF16)


def route(owner, features, cotangent, offset):
    rows = LOW * (2 * CHANNELS + 4)
    return pl.pallas_call(
        route_kernel,
        out_shape=(
            jax.ShapeDtypeStruct((DEVICES, ROWS, SLOTS), BF16),
            jax.ShapeDtypeStruct((1, PARTICLES), jnp.int32),
        ),
        scratch_shapes=[pltpu.VMEM((rows, PARTICLES), BF16)],
        compiler_params=params(30),
        cost_estimate=cost(rows * PARTICLES * HIGH * SLOTS, 3 * 2**20),
    )(owner, features, cotangent, offset)


def network_kernel(feat_ref, cot_ref, in_ref, out_ref, in_t_ref, out_t_ref, local_ref, back_ref, grads_ref):
    step = pl.program_id(0)
    features = feat_ref[...]
    cotangent = cot_ref[...]
    hidden_pre = jnp.dot(in_ref[...], features, preferred_element_type=F32)
    hidden = jax.nn.silu(hidden_pre).astype(BF16)
    local_ref[...] = jnp.dot(out_ref[...], hidden, preferred_element_type=F32)
    hidden_back = jnp.dot(out_t_ref[...], cotangent, preferred_element_type=F32)
    pre_grad = (hidden_back * silu_slope(hidden_pre)).astype(BF16)
    back_ref[...] = jnp.dot(in_t_ref[...], pre_grad, preferred_element_type=F32)
    grad_in = lax.dot_general(features, pre_grad, NT, preferred_element_type=F32)
    grad_out = lax.dot_general(cotangent, hidden, NT, preferred_element_type=F32)
    both = jnp.concatenate([grad_in, grad_out], axis=0)

    @pl.when(step == 0)
    def first():
        grads_ref[...] = both

    @pl.when(step > 0)
    def later():
        grads_ref[...] += both


def network(features, cotangent, mlp_in, mlp_out):
    width = 1024
    hidden = mlp_in.shape[0]

    def whole(rows, columns):
        return pl.BlockSpec((rows, columns), lambda i: (0, 0))

    wide = pl.BlockSpec((CHANNELS, width), lambda i: (0, i))
    return pl.pallas_call(
        network_kernel,
        grid=(PARTICLES // width,),
        in_specs=[
            wide,
            wide,
            whole(hidden, CHANNELS),
            whole(CHANNELS, hidden),
            whole(CHANNELS, hidden),
            whole(hidden, CHANNELS),
        ],
        out_specs=(wide, wide, whole(2 * CHANNELS, hidden)),
        out_shape=(
            jax.ShapeDtypeStruct((CHANNELS, PARTICLES), F32),
            jax.ShapeDtypeStruct((CHANNELS, PARTICLES), F32),
            jax.ShapeDtypeStruct((2 * CHANNELS, hidden), F32),
        ),
        compiler_params=params(16),
        cost_estimate=cost(6 * 128 * 128 * PARTICLES, 2 * 2**20),
    )(features, cotangent, mlp_in, mlp_out, mlp_in.T, mlp_out.T)


def hat(position, at):
    return jnp.maximum(1.0 - jnp.abs(position - at), 0.0)


def places(offset):
    pos_x = offset[0:1] * float(CXD - 1)
    pos_y = jnp.broadcast_to(offset[1:2] * float(CYD - 1), (8, SLOTS))
    pos_z = offset[2:3] * float(GZ - 1)
    depth = lax.broadcasted_iota(jnp.int32, (GZ, SLOTS), 0).astype(F32)
    return pos_x, pos_y, hat(pos_z, depth)


def plane_weights(pos_y, weight_z, first, count):
    rows = []
    for y in [tile + half * TILES for tile in range(first, first + count) for half in range(2)]:
        weight_y = hat(pos_y, float(y))
        for part in range(GZ // 8):
            rows.append(weight_y * weight_z[part * 8 : part * 8 + 8])
    return jnp.concatenate(rows, axis=0).astype(BF16)


def scatter_kernel(blocks, in_ref, out_ref, head_x, tail_x, head_y, tail_y, total):
    step = pl.program_id(0)
    tiles = 2
    sources, placed = [], []
    for j in range(blocks):
        pos_x, pos_y, weight_z = places(in_ref[j, 64:72, :].astype(F32))
        placed.append((pos_y, weight_z))
        parts = []
        for field in range(2):
            values = in_ref[j, field * CHANNELS : (field + 1) * CHANNELS, :].astype(F32)
            for x in range(CXD):
                parts.append((values * hat(pos_x, float(x))).astype(BF16))
        sources.append(jnp.concatenate(parts, axis=0))
    source = jnp.concatenate(sources, axis=1)

    @pl.when(step == 0)
    def first():
        total[...] = jnp.zeros_like(total)

    for tile in range(0, TILES, tiles):
        weights = jnp.concatenate([plane_weights(*place, tile, tiles) for place in placed], axis=1)
        total[:, tile * TILE : (tile + tiles) * TILE] += lax.dot_general(
            source, weights, NT, preferred_element_type=F32
        )

    @pl.when(step == pl.num_programs(0) - 1)
    def last():
        rows = CXD * CHANNELS
        for field in range(2):
            cells = total[field * rows : (field + 1) * rows].astype(BF16)
            out_ref[field] = cells
            head_x[field] = cells[: rows // 2]
            tail_x[field] = cells[rows // 2 :]
            head_y[field] = cells[:, : 2 * TILE]
            tail_y[field] = cells[:, PLANE - 2 * TILE :]


def scatter(arrived):
    blocks = 16
    rows = CXD * CHANNELS
    shapes = [(2, rows, PLANE)] + [(2, rows // 2, PLANE)] * 2 + [(2, rows, 2 * TILE)] * 2
    return pl.pallas_call(
        functools.partial(scatter_kernel, blocks),
        grid=(DEVICES // blocks,),
        in_specs=[pl.BlockSpec((blocks, ROWS, SLOTS), lambda i: (i, 0, 0))],
        out_specs=[pl.BlockSpec(shape, lambda i: (0, 0, 0)) for shape in shapes],
        out_shape=[jax.ShapeDtypeStruct(shape, BF16) for shape in shapes],
        scratch_shapes=[pltpu.VMEM((2 * rows, PLANE), F32)],
        compiler_params=params(24),
        cost_estimate=cost(256 * PLANE * DEVICES * SLOTS, 4 * 2**20),
    )(arrived)


def gather_kernel(blocks, *refs):
    in_ref, grid_ref, out_ref = refs[0], refs[1], refs[-1]
    tiles = 2
    placed = [places(in_ref[j].astype(F32)) for j in range(blocks)]
    total = None
    for tile in range(0, TILES, tiles):
        weights = jnp.concatenate(
            [plane_weights(pos_y, weight_z, tile, tiles) for _, pos_y, weight_z in placed], axis=1
        )
        product = jnp.dot(
            grid_ref[:, tile * TILE : (tile + tiles) * TILE], weights, preferred_element_type=F32
        )
        total = product if total is None else total + product
    for j in range(blocks):
        summed = None
        for x in range(CXD):
            part = total[x * CHANNELS : (x + 1) * CHANNELS, j * SLOTS : (j + 1) * SLOTS]
            part = part * hat(placed[j][0], float(x))
            summed = part if summed is None else summed + part
        if len(refs) == 3:
            out_ref[j, :CHANNELS, :] = summed.astype(BF16)
        else:
            sums = refs[2][j // 2]
            high = sums.astype(BF16).astype(F32)
            rest = sums - high
            upper = lax.broadcasted_iota(jnp.int32, (8, SLOTS), 0) < 4
            if j % 2:
                both = jnp.where(upper, pltpu.roll(high, 4, 0), rest)
            else:
                both = jnp.where(upper, high, pltpu.roll(rest, 4, 0))
            out_ref[j] = jnp.concatenate([summed, both], axis=0).astype(BF16)


def gather(arrived, grids, *parts):
    blocks = 16
    rows = HALF if parts else CHANNELS
    return pl.pallas_call(
        functools.partial(gather_kernel, blocks),
        grid=(DEVICES // blocks,),
        in_specs=[
            pl.BlockSpec((blocks, 8, SLOTS), lambda i: (i, 8, 0)),
            pl.BlockSpec((CXD * CHANNELS, PLANE), lambda i: (0, 0)),
        ]
        + [pl.BlockSpec((blocks // 2, 8, SLOTS), lambda i: (i, 0, 0)) for _ in parts],
        out_specs=pl.BlockSpec((blocks, rows, SLOTS), lambda i: (i, 0, 0)),
        out_shape=jax.ShapeDtypeStruct((DEVICES, HALF, SLOTS), BF16),
        compiler_params=params(24),
        cost_estimate=cost(128 * PLANE * DEVICES * SLOTS, 3 * 2**20),
    )(arrived, grids, *parts)


def attach_kernel(parts_ref, held_ref, out_ref):
    del held_ref
    total = jnp.sum(parts_ref[...].astype(F32), axis=0)
    total = total + pltpu.roll(total, 4, 0)
    high = total.astype(BF16).astype(F32)
    upper = lax.broadcasted_iota(jnp.int32, (8, SLOTS), 0) < 4
    both = jnp.where(upper, high, total - high).astype(BF16)
    out_ref[...] = jnp.broadcast_to(both[None], out_ref.shape)


def attach(returned, payload):
    rows = pl.BlockSpec((DEVICES, 8, SLOTS), lambda i: (0, CHANNELS // 8, 0))
    return pl.pallas_call(
        attach_kernel,
        grid=(1,),
        in_specs=[rows, pl.BlockSpec(memory_space=pl.ANY)],
        out_specs=rows,
        out_shape=jax.ShapeDtypeStruct((DEVICES, HALF, SLOTS), BF16),
        input_output_aliases={1: 0},
        compiler_params=params(8),
        cost_estimate=cost(10**5, 2**19),
    )(returned, payload)


def moved(piece, axis, step):
    count = lax.axis_size(axis)
    pairs = [(i, i + step) for i in range(count) if 0 <= i + step < count]
    return lax.ppermute(piece, axis, pairs)


def corner_kernel(head_y, tail_y, low, high, sides_ref, head_ref, tail_ref):
    half = lax.rem(lax.div(lax.broadcasted_iota(jnp.int32, (1, 2 * TILE), 1), GZ), 2)
    rows = CXD * CHANNELS
    for field in range(2):
        below = jnp.where(half == 1, low[field].astype(F32), tail_y[field].astype(F32))
        above = jnp.where(half == 0, high[field].astype(F32), head_y[field].astype(F32))
        turned = [
            pltpu.roll(side[:, at : at + TILE], GZ, 1) for side in (below, above) for at in (0, TILE)
        ]
        sides = jnp.concatenate(turned, axis=1).astype(BF16)
        sides_ref[field] = sides
        head_ref[field] = sides[: rows // 2]
        tail_ref[field] = sides[rows // 2 :]


def corners(head_y, tail_y, low, high):
    rows = CXD * CHANNELS
    return pl.pallas_call(
        corner_kernel,
        out_shape=[
            jax.ShapeDtypeStruct((2, count, 4 * TILE), BF16)
            for count in (rows, rows // 2, rows // 2)
        ],
        compiler_params=params(8),
        cost_estimate=cost(10**6, 2**20),
    )(head_y, tail_y, low, high)


def conv_kernel(
    own, x_low, x_high, sides, side_low, side_high, w_one, w_back, w_two, w_last, small_ref,
    out_ref, back_ref, grads_ref, zeros, backs, acts, pres, reduced,
):
    spot_a = lax.axis_index("aa")
    spot_b = lax.axis_index("ba")

    def shifted(value, out):
        rows, lanes = value.shape
        depth = lax.rem(lax.broadcasted_iota(jnp.int32, (1, lanes), 1), GZ)
        wide = value.astype(F32)
        before = jnp.where(depth == 0, 0.0, pltpu.roll(wide, 1, 1))
        after = jnp.where(depth == GZ - 1, 0.0, pltpu.roll(wide, lanes - 1, 1))
        out[:rows, :] = before.astype(BF16)
        out[rows : 2 * rows, :] = value
        out[2 * rows :, :] = after.astype(BF16)

    for field, out in enumerate((zeros, backs)):
        planes = jnp.concatenate([x_low[field], own[field], x_high[field]], axis=0)
        edges = jnp.concatenate([side_low[field], sides[field], side_high[field]], axis=0)
        shifted(
            jnp.concatenate([edges[:, : 2 * TILE], planes, edges[:, 2 * TILE :]], axis=1), out
        )

    def convolved(weights, source, lanes):
        total = None
        for step in range(3):
            product = jnp.dot(
                weights[step],
                source[:, step * TILE : step * TILE + lanes],
                preferred_element_type=F32,
            )
            total = product if total is None else total + product
        return total

    pre_one = convolved(w_one, zeros, MID)
    act_back = convolved(w_back, backs, MID)
    plane = lax.div(lax.broadcasted_iota(jnp.int32, (6 * CHANNELS, 1), 0), CHANNELS)
    line = lax.div(lax.broadcasted_iota(jnp.int32, (1, MID), 1), GZ)
    outside_x = ((plane == 0) & (spot_b == 0)) | (
        (plane == CXD + 1) & (spot_b == lax.axis_size("ba") - 1)
    )
    outside_y = ((line == 0) & (spot_a == 0)) | (
        (line == MID // GZ - 1) & (spot_a == lax.axis_size("aa") - 1)
    )
    inside = jnp.where(outside_x, 0.0, 1.0) * jnp.where(outside_y, 0.0, 1.0)
    sigma = jax.nn.sigmoid(pre_one)
    shifted((pre_one * sigma * inside).astype(BF16), acts)
    slope = sigma * (1.0 + pre_one * (1.0 - sigma))
    shifted((act_back * slope * inside).astype(BF16), pres)
    rows = 6 * CHANNELS
    first = rows + CHANNELS
    own_rows = CXD * CHANNELS
    grid_one = own[0].astype(F32) + convolved(w_two, acts, PLANE)
    out_ref[...] = grid_one.astype(BF16)
    back_zero = own[1].astype(F32) + convolved(w_last, pres, PLANE)
    back_ref[...] = back_zero.astype(BF16)

    upstream = (pres[first : first + own_rows, TILE : TILE + PLANE], own[1])
    row_plane = lax.div(lax.broadcasted_iota(jnp.int32, (own_rows, rows), 0), CHANNELS)
    col_plane = lax.div(lax.broadcasted_iota(jnp.int32, (own_rows, rows), 1), CHANNELS)
    for conv in range(2):
        for step_y in range(3):
            for step_z in range(3):
                if conv == 0:
                    start = step_z * 8 * CHANNELS + CHANNELS
                    at = (step_y + 1) * TILE
                    field = zeros[start : start + rows, at : at + PLANE]
                else:
                    at = step_y * TILE
                    field = acts[step_z * rows : (step_z + 1) * rows, at : at + PLANE]
                product = lax.dot_general(upstream[conv], field, NT, preferred_element_type=F32)
                for step_x in range(3):
                    kept = jnp.where(col_plane == row_plane + step_x, product, 0.0)
                    folded = kept[:CHANNELS]
                    for x in range(1, CXD):
                        folded = folded + kept[x * CHANNELS : (x + 1) * CHANNELS]
                    at = (conv * 27 + step_x * 9 + step_y * 3 + step_z) * CHANNELS
                    reduced[at : at + CHANNELS, :] = folded
    quarter = 2 * 27 * CHANNELS // 4
    total = None
    for part in range(4):
        source = lax.broadcasted_iota(jnp.int32, (rows, 128), 0)
        target = lax.broadcasted_iota(jnp.int32, (rows, 128), 1)
        chosen = (target == lax.rem(source, CHANNELS) + part * CHANNELS).astype(F32)
        product = jnp.dot(
            reduced[part * quarter : (part + 1) * quarter, :],
            chosen,
            preferred_element_type=F32,
            precision=lax.Precision.HIGHEST,
        )
        total = product if total is None else total + product
    small = small_ref[...]
    filler = jnp.zeros((4 * DEVICES - quarter - small.shape[0], SLOTS), F32)
    grads_ref[:quarter] = total
    grads_ref[quarter:] = jnp.concatenate([small, filler], axis=0)


def band(kernel, planes):
    taps = kernel.reshape(3, 3, 3, CHANNELS, CHANNELS)
    taps = jnp.transpose(taps, (1, 3, 2, 0, 4))
    taps = jnp.pad(taps, ((0, 0), (0, 0), (0, 0), (0, planes - 1), (0, 0)))
    return taps.reshape(3, CHANNELS, 3 * (planes + 2) * CHANNELS)


def toeplitz_kernel(*refs):
    for band_ref, out_ref in zip(refs[:4], refs[4:]):
        for step in range(3):
            first = band_ref[step].astype(F32)
            for x in range(out_ref.shape[1] // CHANNELS):
                moved = first if x == 0 else pltpu.roll(first, x * CHANNELS, 1)
                out_ref[step, x * CHANNELS : (x + 1) * CHANNELS, :] = moved.astype(BF16)


def toeplitz(kernel_one, kernel_two):
    bands = (
        band(kernel_one, 6),
        band(flipped(kernel_two), 6),
        band(kernel_two, 4),
        band(flipped(kernel_one), 4),
    )
    return pl.pallas_call(
        toeplitz_kernel,
        out_shape=[
            jax.ShapeDtypeStruct((3, planes * CHANNELS, 3 * (planes + 2) * CHANNELS), BF16)
            for planes in (6, 6, 4, 4)
        ],
        compiler_params=params(16),
        cost_estimate=cost(10**7, 4 * 2**20),
    )(*bands)


def conv_block(grids, edges, weights, small):
    rows_one = 3 * 8 * CHANNELS
    rows_two = 3 * 6 * CHANNELS
    shape = jax.ShapeDtypeStruct((CXD * CHANNELS, PLANE), BF16)
    return pl.pallas_call(
        conv_kernel,
        out_shape=(shape, shape, jax.ShapeDtypeStruct((4 * DEVICES, SLOTS), F32)),
        scratch_shapes=[
            pltpu.VMEM((rows_one, WIDE), BF16),
            pltpu.VMEM((rows_one, WIDE), BF16),
            pltpu.VMEM((rows_two, MID), BF16),
            pltpu.VMEM((rows_two, MID), BF16),
            pltpu.VMEM((2 * 27 * CHANNELS, 6 * CHANNELS), F32),
        ],
        compiler_params=params(32),
        cost_estimate=cost(6 * 10**9, 8 * 2**20),
    )(grids, *edges, *weights, small)


def unroute_kernel(ret_ref, slot_ref, owner_ref, local_ref, out_ref, *refs):
    rows = CHANNELS
    table = refs[-1]
    for high in range(HIGH):
        for low in range(LOW):
            table[low * rows : (low + 1) * rows, high * SLOTS : (high + 1) * SLOTS] = ret_ref[
                high * LOW + low, :rows, :
            ]
    width = 512
    for step in range(PARTICLES // width):
        lanes = slice(step * width, (step + 1) * width)
        slot_ids = lax.broadcasted_iota(jnp.int32, (HIGH * SLOTS, width), 0)
        hot = (slot_ids == slot_ref[:, lanes]).astype(F32).astype(BF16)
        found = jnp.dot(table[...], hot, preferred_element_type=F32)
        low = lax.rem(owner_ref[:, lanes], LOW)
        mine = None
        for group in range(LOW):
            part = jnp.where(low == group, found[group * rows : (group + 1) * rows], 0.0)
            mine = part if mine is None else mine + part
        out_ref[:, lanes] = (mine + local_ref[:, lanes]).astype(BF16)
    if len(refs) == 1:
        return

    kernels_ref, in_ref, mlp_ref = refs[:3]
    halves = ret_ref[:, rows:, :].astype(F32)
    summed = (halves + pltpu.roll(halves, 4, 1)).reshape(DEVICES // 2, 2, 8, SLOTS)
    upper = lax.broadcasted_iota(jnp.int32, (DEVICES // 2, 8, SLOTS), 1) < 4
    summed = jnp.where(upper, summed[:, 0], summed[:, 1]).reshape(4 * DEVICES, SLOTS)
    quarter = 2 * 27 * CHANNELS // 4
    for part in range(4):
        turned = summed[:quarter]
        if part:
            turned = pltpu.roll(turned, 128 - part * CHANNELS, 1)
        kernels_ref[part * quarter : (part + 1) * quarter, :] = turned[:, :CHANNELS]
    in_ref[...] = summed[quarter : quarter + CHANNELS]
    mlp_ref[...] = summed[quarter + CHANNELS : quarter + 2 * CHANNELS]


def unroute(returned, slot, owner, addend, sums):
    shapes = [jax.ShapeDtypeStruct((CHANNELS, PARTICLES), BF16)]
    if sums:
        shapes += [
            jax.ShapeDtypeStruct((2 * 27 * CHANNELS, CHANNELS), F32),
            jax.ShapeDtypeStruct((CHANNELS, 128), F32),
            jax.ShapeDtypeStruct((CHANNELS, 128), F32),
        ]
    return pl.pallas_call(
        unroute_kernel,
        out_shape=shapes,
        scratch_shapes=[pltpu.VMEM((LOW * CHANNELS, HIGH * SLOTS), BF16)],
        compiler_params=params(20),
        cost_estimate=cost(512 * 1024 * PARTICLES, 3 * 2**20),
    )(returned, slot, owner, addend)


def exchanged(blocks):
    return lax.all_to_all(blocks, ("aa", "ba"), split_axis=0, concat_axis=0, tiled=True)


def local(features, cotangent, owner, offset, kernel_one, kernel_two, mlp_in, mlp_out):
    owner = owner.reshape(1, PARTICLES)
    outgoing, slot = route(owner, features, cotangent, offset)
    arrived = exchanged(outgoing)
    local_out, local_back, small = network(features, cotangent, mlp_in, mlp_out)
    weights = toeplitz(kernel_one, kernel_two)
    arrived, weights, small = lax.optimization_barrier((arrived, weights, small))
    grids, head_x, tail_x, head_y, tail_y = scatter(arrived)
    x_low, x_high = moved(tail_x, "ba", 1), moved(head_x, "ba", -1)
    y_low, y_high = moved(tail_y, "aa", 1), moved(head_y, "aa", -1)
    sides, side_head, side_tail = corners(head_y, tail_y, y_low, y_high)
    side_low, side_high = moved(side_tail, "ba", 1), moved(side_head, "ba", -1)
    edges = (x_low, x_high, sides, side_low, side_high)
    grid_one, back_zero, parts = conv_block(grids, edges, weights, small)
    first = exchanged(gather(arrived, grid_one, parts.reshape(DEVICES // 2, 8, SLOTS)))
    second = exchanged(attach(first, gather(arrived, back_zero)))
    (particle_out,) = unroute(first, slot, owner, local_out, False)
    feat_grad, grad_kernels, grad_in, grad_out = unroute(second, slot, owner, local_back, True)
    grad_kernels = grad_kernels.reshape(2, 27, CHANNELS, CHANNELS)
    return particle_out, feat_grad, grad_kernels, grad_in.T, grad_out


def solution(mesh):
    in_specs = (
        P(None, ("aa", "ba")),
        P(None, ("aa", "ba")),
        P(("aa", "ba"), None),
        P(None, ("aa", "ba")),
        P(),
        P(),
        P(),
        P(),
    )
    out_specs = (P(None, ("aa", "ba")), P(None, ("aa", "ba")), P(), P(), P())
    return jax.shard_map(local, mesh=mesh, in_specs=in_specs, out_specs=out_specs, check_vma=False)
```

```python
import functools

import jax
import jax.numpy as jnp
from jax import lax
from jax.experimental import pallas as pl
from jax.experimental.pallas import tpu as pltpu
from jax.sharding import PartitionSpec as P

F32 = jnp.float32
BF16 = jnp.bfloat16
NT = (((1,), (1,)), ((), ()))

DEVICES = 128
SLOTS = 128
PARTICLES = 4096
CHANNELS = 32
GZ = 64
CXD = 4
CYD = 32
PLANE = CYD * GZ
ROWS = 72
HALF = 40
TILE = 2 * GZ
TILES = PLANE // TILE
WIDE = PLANE + 4 * TILE
MID = PLANE + 2 * TILE
LOW = 16
HIGH = DEVICES // LOW


def params(mebibytes):
    return pltpu.CompilerParams(vmem_limit_bytes=mebibytes * 2**20)


def cost(macs, moved):
    return pl.CostEstimate(flops=2 * macs, bytes_accessed=moved, transcendentals=0)


def rows16(row):
    return jnp.broadcast_to(row, (16, row.shape[1]))


def silu_slope(value):
    sigma_value = jax.nn.sigmoid(value)
    return sigma_value * (1.0 + value * (1.0 - sigma_value))


def flipped(kernel):
    return jnp.transpose(kernel[::-1], (0, 2, 1))


def route_kernel(owner_ref, feat_ref, cot_ref, off_ref, out_ref, slot_ref, spread):
    block = 256
    owner_ids = lax.broadcasted_iota(jnp.int32, (DEVICES, block), 0)
    before = lax.broadcasted_iota(jnp.int32, (block, block + 128), 0)
    after = lax.broadcasted_iota(jnp.int32, (block, block + 128), 1)
    prefix = ((before < after) | (after >= block)).astype(F32).astype(BF16)
    base = jnp.zeros((DEVICES, 128), F32)
    ranks = []
    for number in range(PARTICLES // block):
        hot = (owner_ids == owner_ref[:, number * block : (number + 1) * block]).astype(F32)
        counted = jnp.dot(hot.astype(BF16), prefix, preferred_element_type=F32)
        earlier = counted[:, :block] + jnp.concatenate([base, base], axis=1)
        ranks.append(jnp.sum(hot * earlier, axis=0, keepdims=True))
        base = base + counted[:, block:]
    rank = jnp.concatenate(ranks, axis=1).astype(jnp.int32)
    owner = owner_ref[...]
    low = lax.rem(owner, LOW)
    slot = lax.div(owner, LOW) * SLOTS + rank
    slot_ref[...] = slot
    for group in range(LOW):
        mask = rows16((low == group).astype(F32)).astype(BF16)
        for field, source in enumerate((feat_ref, cot_ref)):
            for part in range(0, CHANNELS, 16):
                at = group * 2 * CHANNELS + field * CHANNELS + part
                spread[at : at + 16, :] = source[part : part + 16, :] * mask
    tail = LOW * 2 * CHANNELS
    offset = off_ref[...].astype(F32)
    nothing = jnp.zeros((1, PARTICLES), F32)
    offset = jnp.concatenate([offset, nothing, offset, nothing], axis=0)
    line = lax.div(lax.broadcasted_iota(jnp.int32, (8, PARTICLES), 0), 4)
    for group in range(0, LOW, 4):
        parts = [jnp.where(low == group + pair + line, offset, 0.0) for pair in (0, 2)]
        spread[tail + group * 4 : tail + group * 4 + 16, :] = jnp.concatenate(
            parts, axis=0
        ).astype(BF16)
    width = 256
    for step in range(HIGH * SLOTS // width):
        slot_ids = lax.broadcasted_iota(jnp.int32, (width, PARTICLES), 0) + step * width
        hot = (slot_ids == slot).astype(F32).astype(BF16)
        placed = lax.dot_general(spread[...], hot, NT, preferred_element_type=F32)
        for part in range(width // SLOTS):
            high = step * (width // SLOTS) + part
            lanes = slice(part * SLOTS, (part + 1) * SLOTS)
            for group in range(LOW):
                values = placed[group * 2 * CHANNELS : (group + 1) * 2 * CHANNELS, lanes]
                at = tail + group // 2 * 8
                where = placed[at : at + 8, lanes]
                if group % 2:
                    where = pltpu.roll(where, 4, 0)
                out_ref[high * LOW + group] = jnp.concatenate([values, where], axis=0).astype(BF16)


def route(owner, features, cotangent, offset):
    rows = LOW * (2 * CHANNELS + 4)
    return pl.pallas_call(
        route_kernel,
        out_shape=(
            jax.ShapeDtypeStruct((DEVICES, ROWS, SLOTS), BF16),
            jax.ShapeDtypeStruct((1, PARTICLES), jnp.int32),
        ),
        scratch_shapes=[pltpu.VMEM((rows, PARTICLES), BF16)],
        compiler_params=params(60),
        cost_estimate=cost(rows * PARTICLES * HIGH * SLOTS, 3 * 2**20),
    )(owner, features, cotangent, offset)


def network_kernel(feat_ref, cot_ref, in_ref, out_ref, in_t_ref, out_t_ref, local_ref, back_ref, grads_ref):
    step = pl.program_id(0)
    features = feat_ref[...]
    cotangent = cot_ref[...]
    hidden_pre = jnp.dot(in_ref[...], features, preferred_element_type=F32)
    hidden = jax.nn.silu(hidden_pre).astype(BF16)
    local_ref[...] = jnp.dot(out_ref[...], hidden, preferred_element_type=F32)
    hidden_back = jnp.dot(out_t_ref[...], cotangent, preferred_element_type=F32)
    pre_grad = (hidden_back * silu_slope(hidden_pre)).astype(BF16)
    back_ref[...] = jnp.dot(in_t_ref[...], pre_grad, preferred_element_type=F32)
    grad_in = lax.dot_general(features, pre_grad, NT, preferred_element_type=F32)
    grad_out = lax.dot_general(cotangent, hidden, NT, preferred_element_type=F32)
    both = jnp.concatenate([grad_in, grad_out], axis=0)

    @pl.when(step == 0)
    def first():
        grads_ref[...] = both

    @pl.when(step > 0)
    def later():
        grads_ref[...] += both


def network(features, cotangent, mlp_in, mlp_out):
    width = 1024
    hidden = mlp_in.shape[0]

    def whole(rows, columns):
        return pl.BlockSpec((rows, columns), lambda i: (0, 0))

    wide = pl.BlockSpec((CHANNELS, width), lambda i: (0, i))
    return pl.pallas_call(
        network_kernel,
        grid=(PARTICLES // width,),
        in_specs=[
            wide,
            wide,
            whole(hidden, CHANNELS),
            whole(CHANNELS, hidden),
            whole(CHANNELS, hidden),
            whole(hidden, CHANNELS),
        ],
        out_specs=(wide, wide, whole(2 * CHANNELS, hidden)),
        out_shape=(
            jax.ShapeDtypeStruct((CHANNELS, PARTICLES), F32),
            jax.ShapeDtypeStruct((CHANNELS, PARTICLES), F32),
            jax.ShapeDtypeStruct((2 * CHANNELS, hidden), F32),
        ),
        compiler_params=params(16),
        cost_estimate=cost(6 * 128 * 128 * PARTICLES, 2 * 2**20),
    )(features, cotangent, mlp_in, mlp_out, mlp_in.T, mlp_out.T)


def hat(position, at):
    return jnp.maximum(1.0 - jnp.abs(position - at), 0.0)


def places(offset):
    pos_x = offset[0:1] * float(CXD - 1)
    pos_y = jnp.broadcast_to(offset[1:2] * float(CYD - 1), (8, SLOTS))
    pos_z = offset[2:3] * float(GZ - 1)
    depth = lax.broadcasted_iota(jnp.int32, (GZ, SLOTS), 0).astype(F32)
    return pos_x, pos_y, hat(pos_z, depth)


def plane_weights(pos_y, weight_z, first, count):
    rows = []
    for y in [tile + half * TILES for tile in range(first, first + count) for half in range(2)]:
        weight_y = hat(pos_y, float(y))
        for part in range(GZ // 8):
            rows.append(weight_y * weight_z[part * 8 : part * 8 + 8])
    return jnp.concatenate(rows, axis=0).astype(BF16)


def scatter_kernel(blocks, in_ref, out_ref, head_x, tail_x, head_y, tail_y, total):
    step = pl.program_id(0)
    tiles = 2
    sources, placed = [], []
    for j in range(blocks):
        pos_x, pos_y, weight_z = places(in_ref[j, 64:72, :].astype(F32))
        placed.append((pos_y, weight_z))
        parts = []
        for field in range(2):
            values = in_ref[j, field * CHANNELS : (field + 1) * CHANNELS, :].astype(F32)
            for x in range(CXD):
                parts.append((values * hat(pos_x, float(x))).astype(BF16))
        sources.append(jnp.concatenate(parts, axis=0))
    source = jnp.concatenate(sources, axis=1)

    @pl.when(step == 0)
    def first():
        total[...] = jnp.zeros_like(total)

    for tile in range(0, TILES, tiles):
        weights = jnp.concatenate([plane_weights(*place, tile, tiles) for place in placed], axis=1)
        total[:, tile * TILE : (tile + tiles) * TILE] += lax.dot_general(
            source, weights, NT, preferred_element_type=F32
        )

    @pl.when(step == pl.num_programs(0) - 1)
    def last():
        rows = CXD * CHANNELS
        for field in range(2):
            cells = total[field * rows : (field + 1) * rows].astype(BF16)
            out_ref[field] = cells
            head_x[field] = cells[: rows // 2]
            tail_x[field] = cells[rows // 2 :]
            head_y[field] = cells[:, : 2 * TILE]
            tail_y[field] = cells[:, PLANE - 2 * TILE :]


def scatter(arrived):
    blocks = 32
    rows = CXD * CHANNELS
    shapes = [(2, rows, PLANE)] + [(2, rows // 2, PLANE)] * 2 + [(2, rows, 2 * TILE)] * 2
    return pl.pallas_call(
        functools.partial(scatter_kernel, blocks),
        grid=(DEVICES // blocks,),
        in_specs=[pl.BlockSpec((blocks, ROWS, SLOTS), lambda i: (i, 0, 0))],
        out_specs=[pl.BlockSpec(shape, lambda i: (0, 0, 0)) for shape in shapes],
        out_shape=[jax.ShapeDtypeStruct(shape, BF16) for shape in shapes],
        scratch_shapes=[pltpu.VMEM((2 * rows, PLANE), F32)],
        compiler_params=params(24),
        cost_estimate=cost(256 * PLANE * DEVICES * SLOTS, 4 * 2**20),
    )(arrived)


def gather_kernel(blocks, *refs):
    in_ref, grid_ref, out_ref = refs[0], refs[1], refs[-1]
    tiles = 2
    placed = [places(in_ref[j].astype(F32)) for j in range(blocks)]
    total = None
    for tile in range(0, TILES, tiles):
        weights = jnp.concatenate(
            [plane_weights(pos_y, weight_z, tile, tiles) for _, pos_y, weight_z in placed], axis=1
        )
        product = jnp.dot(
            grid_ref[:, tile * TILE : (tile + tiles) * TILE], weights, preferred_element_type=F32
        )
        total = product if total is None else total + product
    for j in range(blocks):
        summed = None
        for x in range(CXD):
            part = total[x * CHANNELS : (x + 1) * CHANNELS, j * SLOTS : (j + 1) * SLOTS]
            part = part * hat(placed[j][0], float(x))
            summed = part if summed is None else summed + part
        if len(refs) == 3:
            out_ref[j, :CHANNELS, :] = summed.astype(BF16)
        else:
            sums = refs[2][j // 2]
            high = sums.astype(BF16).astype(F32)
            rest = sums - high
            upper = lax.broadcasted_iota(jnp.int32, (8, SLOTS), 0) < 4
            if j % 2:
                both = jnp.where(upper, pltpu.roll(high, 4, 0), rest)
            else:
                both = jnp.where(upper, high, pltpu.roll(rest, 4, 0))
            out_ref[j] = jnp.concatenate([summed, both], axis=0).astype(BF16)


def gather(arrived, grids, *parts):
    blocks = 16
    rows = HALF if parts else CHANNELS
    return pl.pallas_call(
        functools.partial(gather_kernel, blocks),
        grid=(DEVICES // blocks,),
        in_specs=[
            pl.BlockSpec((blocks, 8, SLOTS), lambda i: (i, 8, 0)),
            pl.BlockSpec((CXD * CHANNELS, PLANE), lambda i: (0, 0)),
        ]
        + [pl.BlockSpec((blocks // 2, 8, SLOTS), lambda i: (i, 0, 0)) for _ in parts],
        out_specs=pl.BlockSpec((blocks, rows, SLOTS), lambda i: (i, 0, 0)),
        out_shape=jax.ShapeDtypeStruct((DEVICES, HALF, SLOTS), BF16),
        compiler_params=params(24),
        cost_estimate=cost(128 * PLANE * DEVICES * SLOTS, 3 * 2**20),
    )(arrived, grids, *parts)


def attach_kernel(parts_ref, held_ref, out_ref):
    del held_ref
    total = jnp.sum(parts_ref[...].astype(F32), axis=0)
    total = total + pltpu.roll(total, 4, 0)
    high = total.astype(BF16).astype(F32)
    upper = lax.broadcasted_iota(jnp.int32, (8, SLOTS), 0) < 4
    both = jnp.where(upper, high, total - high).astype(BF16)
    out_ref[...] = jnp.broadcast_to(both[None], out_ref.shape)


def attach(returned, payload):
    rows = pl.BlockSpec((DEVICES, 8, SLOTS), lambda i: (0, CHANNELS // 8, 0))
    return pl.pallas_call(
        attach_kernel,
        grid=(1,),
        in_specs=[rows, pl.BlockSpec(memory_space=pl.ANY)],
        out_specs=rows,
        out_shape=jax.ShapeDtypeStruct((DEVICES, HALF, SLOTS), BF16),
        input_output_aliases={1: 0},
        compiler_params=params(8),
        cost_estimate=cost(10**5, 2**19),
    )(returned, payload)


def moved(piece, axis, step):
    count = lax.axis_size(axis)
    pairs = [(i, i + step) for i in range(count) if 0 <= i + step < count]
    return lax.ppermute(piece, axis, pairs)


def corner_kernel(head_y, tail_y, low, high, sides_ref, head_ref, tail_ref):
    half = lax.rem(lax.div(lax.broadcasted_iota(jnp.int32, (1, 2 * TILE), 1), GZ), 2)
    rows = CXD * CHANNELS
    for field in range(2):
        below = jnp.where(half == 1, low[field].astype(F32), tail_y[field].astype(F32))
        above = jnp.where(half == 0, high[field].astype(F32), head_y[field].astype(F32))
        turned = [
            pltpu.roll(side[:, at : at + TILE], GZ, 1) for side in (below, above) for at in (0, TILE)
        ]
        sides = jnp.concatenate(turned, axis=1).astype(BF16)
        sides_ref[field] = sides
        head_ref[field] = sides[: rows // 2]
        tail_ref[field] = sides[rows // 2 :]


def corners(head_y, tail_y, low, high):
    rows = CXD * CHANNELS
    return pl.pallas_call(
        corner_kernel,
        out_shape=[
            jax.ShapeDtypeStruct((2, count, 4 * TILE), BF16)
            for count in (rows, rows // 2, rows // 2)
        ],
        compiler_params=params(8),
        cost_estimate=cost(10**6, 2**20),
    )(head_y, tail_y, low, high)


def shifted(value, out):
    rows, lanes = value.shape
    depth = lax.rem(lax.broadcasted_iota(jnp.int32, (1, lanes), 1), GZ)
    wide = value.astype(F32)
    before = jnp.where(depth == 0, 0.0, pltpu.roll(wide, 1, 1))
    after = jnp.where(depth == GZ - 1, 0.0, pltpu.roll(wide, lanes - 1, 1))
    out[:rows, :] = before.astype(BF16)
    out[rows : 2 * rows, :] = value
    out[2 * rows :, :] = after.astype(BF16)


def convolved(weights, source, lanes):
    total = None
    for step in range(3):
        product = jnp.dot(
            weights[step],
            source[:, step * TILE : step * TILE + lanes],
            preferred_element_type=F32,
        )
        total = product if total is None else total + product
    return total


def conv_kernel(
    own, x_low, x_high, sides, side_low, side_high, w_one, w_back, w_two, small_ref,
    out_ref, pre_ref, grads_ref, zeros, backs, acts, reduced,
):
    spot_a = lax.axis_index("aa")
    spot_b = lax.axis_index("ba")

    for field, out in enumerate((zeros, backs)):
        planes = jnp.concatenate([x_low[field], own[field], x_high[field]], axis=0)
        edges = jnp.concatenate([side_low[field], sides[field], side_high[field]], axis=0)
        shifted(
            jnp.concatenate([edges[:, : 2 * TILE], planes, edges[:, 2 * TILE :]], axis=1), out
        )

    pre_one = convolved(w_one, zeros, MID)
    act_back = convolved(w_back, backs, MID)
    plane = lax.div(lax.broadcasted_iota(jnp.int32, (6 * CHANNELS, 1), 0), CHANNELS)
    line = lax.div(lax.broadcasted_iota(jnp.int32, (1, MID), 1), GZ)
    outside_x = ((plane == 0) & (spot_b == 0)) | (
        (plane == CXD + 1) & (spot_b == lax.axis_size("ba") - 1)
    )
    outside_y = ((line == 0) & (spot_a == 0)) | (
        (line == MID // GZ - 1) & (spot_a == lax.axis_size("aa") - 1)
    )
    inside = jnp.where(outside_x, 0.0, 1.0) * jnp.where(outside_y, 0.0, 1.0)
    sigma = jax.nn.sigmoid(pre_one)
    shifted((pre_one * sigma * inside).astype(BF16), acts)
    slope = sigma * (1.0 + pre_one * (1.0 - sigma))
    pre_back = (act_back * slope * inside).astype(BF16)
    pre_ref[...] = pre_back
    rows = 6 * CHANNELS
    own_rows = CXD * CHANNELS
    grid_one = own[0].astype(F32) + convolved(w_two, acts, PLANE)
    out_ref[...] = grid_one.astype(BF16)

    upstream = (pre_back[CHANNELS : CHANNELS + own_rows, TILE : TILE + PLANE], own[1])
    row_plane = lax.div(lax.broadcasted_iota(jnp.int32, (own_rows, rows), 0), CHANNELS)
    col_plane = lax.div(lax.broadcasted_iota(jnp.int32, (own_rows, rows), 1), CHANNELS)
    for conv in range(2):
        for step_y in range(3):
            for step_z in range(3):
                if conv == 0:
                    start = step_z * 8 * CHANNELS + CHANNELS
                    at = (step_y + 1) * TILE
                    field = zeros[start : start + rows, at : at + PLANE]
                else:
                    at = step_y * TILE
                    field = acts[step_z * rows : (step_z + 1) * rows, at : at + PLANE]
                product = lax.dot_general(upstream[conv], field, NT, preferred_element_type=F32)
                for step_x in range(3):
                    kept = jnp.where(col_plane == row_plane + step_x, product, 0.0)
                    folded = kept[:CHANNELS]
                    for x in range(1, CXD):
                        folded = folded + kept[x * CHANNELS : (x + 1) * CHANNELS]
                    at = (conv * 27 + step_x * 9 + step_y * 3 + step_z) * CHANNELS
                    reduced[at : at + CHANNELS, :] = folded
    quarter = 2 * 27 * CHANNELS // 4
    total = None
    for part in range(4):
        source = lax.broadcasted_iota(jnp.int32, (rows, 128), 0)
        target = lax.broadcasted_iota(jnp.int32, (rows, 128), 1)
        chosen = (target == lax.rem(source, CHANNELS) + part * CHANNELS).astype(F32)
        product = jnp.dot(
            reduced[part * quarter : (part + 1) * quarter, :],
            chosen,
            preferred_element_type=F32,
            precision=lax.Precision.HIGHEST,
        )
        total = product if total is None else total + product
    small = small_ref[...]
    filler = jnp.zeros((4 * DEVICES - quarter - small.shape[0], SLOTS), F32)
    grads_ref[:quarter] = total
    grads_ref[quarter:] = jnp.concatenate([small, filler], axis=0)


def band(kernel, planes):
    taps = kernel.reshape(3, 3, 3, CHANNELS, CHANNELS)
    taps = jnp.transpose(taps, (1, 3, 2, 0, 4))
    taps = jnp.pad(taps, ((0, 0), (0, 0), (0, 0), (0, planes - 1), (0, 0)))
    return taps.reshape(3, CHANNELS, 3 * (planes + 2) * CHANNELS)


def toeplitz_kernel(*refs):
    for band_ref, out_ref in zip(refs[:4], refs[4:]):
        for step in range(3):
            first = band_ref[step].astype(F32)
            for x in range(out_ref.shape[1] // CHANNELS):
                moved = first if x == 0 else pltpu.roll(first, x * CHANNELS, 1)
                out_ref[step, x * CHANNELS : (x + 1) * CHANNELS, :] = moved.astype(BF16)


def toeplitz(kernel_one, kernel_two):
    bands = (
        band(kernel_one, 6),
        band(flipped(kernel_two), 6),
        band(kernel_two, 4),
        band(flipped(kernel_one), 4),
    )
    return pl.pallas_call(
        toeplitz_kernel,
        out_shape=[
            jax.ShapeDtypeStruct((3, planes * CHANNELS, 3 * (planes + 2) * CHANNELS), BF16)
            for planes in (6, 6, 4, 4)
        ],
        compiler_params=params(16),
        cost_estimate=cost(10**7, 4 * 2**20),
    )(*bands)


def conv_block(grids, edges, weights, small):
    rows_one = 3 * 8 * CHANNELS
    rows_two = 3 * 6 * CHANNELS
    shape = jax.ShapeDtypeStruct((CXD * CHANNELS, PLANE), BF16)
    return pl.pallas_call(
        conv_kernel,
        out_shape=(
            shape,
            jax.ShapeDtypeStruct((6 * CHANNELS, MID), BF16),
            jax.ShapeDtypeStruct((4 * DEVICES, SLOTS), F32),
        ),
        scratch_shapes=[
            pltpu.VMEM((rows_one, WIDE), BF16),
            pltpu.VMEM((rows_one, WIDE), BF16),
            pltpu.VMEM((rows_two, MID), BF16),
            pltpu.VMEM((2 * 27 * CHANNELS, 6 * CHANNELS), F32),
        ],
        compiler_params=params(32),
        cost_estimate=cost(6 * 10**9, 8 * 2**20),
    )(grids, *edges, *weights[:3], small)


def last_kernel(own, pre_ref, w_last, out_ref, pres):
    shifted(pre_ref[...], pres)
    out_ref[...] = (own[0].astype(F32) + convolved(w_last, pres, PLANE)).astype(BF16)


def last_conv(grids, pre_back, weight):
    rows = CXD * CHANNELS
    return pl.pallas_call(
        last_kernel,
        grid=(1,),
        in_specs=[
            pl.BlockSpec((1, rows, PLANE), lambda i: (1, 0, 0)),
            pl.BlockSpec(pre_back.shape, lambda i: (0, 0)),
            pl.BlockSpec(weight.shape, lambda i: (0, 0, 0)),
        ],
        out_specs=pl.BlockSpec((rows, PLANE), lambda i: (0, 0)),
        out_shape=jax.ShapeDtypeStruct((rows, PLANE), BF16),
        scratch_shapes=[pltpu.VMEM((3 * 6 * CHANNELS, MID), BF16)],
        compiler_params=params(16),
        cost_estimate=cost(10**9, 2 * 2**20),
    )(grids, pre_back, weight)


def unroute_kernel(ret_ref, slot_ref, owner_ref, local_ref, out_ref, *refs):
    rows = CHANNELS
    table = refs[-1]
    for high in range(HIGH):
        for low in range(LOW):
            table[low * rows : (low + 1) * rows, high * SLOTS : (high + 1) * SLOTS] = ret_ref[
                high * LOW + low, :rows, :
            ]
    width = 512
    for step in range(PARTICLES // width):
        lanes = slice(step * width, (step + 1) * width)
        slot_ids = lax.broadcasted_iota(jnp.int32, (HIGH * SLOTS, width), 0)
        hot = (slot_ids == slot_ref[:, lanes]).astype(F32).astype(BF16)
        found = jnp.dot(table[...], hot, preferred_element_type=F32)
        low = lax.rem(owner_ref[:, lanes], LOW)
        mine = None
        for group in range(LOW):
            part = jnp.where(low == group, found[group * rows : (group + 1) * rows], 0.0)
            mine = part if mine is None else mine + part
        out_ref[:, lanes] = (mine + local_ref[:, lanes]).astype(BF16)
    if len(refs) == 1:
        return

    kernels_ref, in_ref, mlp_ref = refs[:3]
    halves = ret_ref[:, rows:, :].astype(F32)
    summed = (halves + pltpu.roll(halves, 4, 1)).reshape(DEVICES // 2, 2, 8, SLOTS)
    upper = lax.broadcasted_iota(jnp.int32, (DEVICES // 2, 8, SLOTS), 1) < 4
    summed = jnp.where(upper, summed[:, 0], summed[:, 1]).reshape(4 * DEVICES, SLOTS)
    quarter = 2 * 27 * CHANNELS // 4
    for part in range(4):
        turned = summed[:quarter]
        if part:
            turned = pltpu.roll(turned, 128 - part * CHANNELS, 1)
        kernels_ref[part * quarter : (part + 1) * quarter, :] = turned[:, :CHANNELS]
    in_ref[...] = summed[quarter : quarter + CHANNELS]
    mlp_ref[...] = summed[quarter + CHANNELS : quarter + 2 * CHANNELS]


def unroute(returned, slot, owner, addend, sums):
    shapes = [jax.ShapeDtypeStruct((CHANNELS, PARTICLES), BF16)]
    if sums:
        shapes += [
            jax.ShapeDtypeStruct((2 * 27 * CHANNELS, CHANNELS), F32),
            jax.ShapeDtypeStruct((CHANNELS, 128), F32),
            jax.ShapeDtypeStruct((CHANNELS, 128), F32),
        ]
    return pl.pallas_call(
        unroute_kernel,
        out_shape=shapes,
        scratch_shapes=[pltpu.VMEM((LOW * CHANNELS, HIGH * SLOTS), BF16)],
        compiler_params=params(20),
        cost_estimate=cost(512 * 1024 * PARTICLES, 3 * 2**20),
    )(returned, slot, owner, addend)


def exchanged(blocks):
    return lax.all_to_all(blocks, ("aa", "ba"), split_axis=0, concat_axis=0, tiled=True)


def local(features, cotangent, owner, offset, kernel_one, kernel_two, mlp_in, mlp_out):
    owner = owner.reshape(1, PARTICLES)
    outgoing, slot = route(owner, features, cotangent, offset)
    arrived = exchanged(outgoing)
    local_out, local_back, small = network(features, cotangent, mlp_in, mlp_out)
    weights = toeplitz(kernel_one, kernel_two)
    arrived, weights, small = lax.optimization_barrier((arrived, weights, small))
    grids, head_x, tail_x, head_y, tail_y = scatter(arrived)
    x_low, x_high = moved(tail_x, "ba", 1), moved(head_x, "ba", -1)
    y_low, y_high = moved(tail_y, "aa", 1), moved(head_y, "aa", -1)
    sides, side_head, side_tail = corners(head_y, tail_y, y_low, y_high)
    side_low, side_high = moved(side_tail, "ba", 1), moved(side_head, "ba", -1)
    edges = (x_low, x_high, sides, side_low, side_high)
    grid_one, pre_back, parts = conv_block(grids, edges, weights, small)
    first = exchanged(gather(arrived, grid_one, parts.reshape(DEVICES // 2, 8, SLOTS)))
    back_zero = last_conv(grids, pre_back, weights[3])
    second = exchanged(attach(first, gather(arrived, back_zero)))
    (particle_out,) = unroute(first, slot, owner, local_out, False)
    feat_grad, grad_kernels, grad_in, grad_out = unroute(second, slot, owner, local_back, True)
    grad_kernels = grad_kernels.reshape(2, 27, CHANNELS, CHANNELS)
    return particle_out, feat_grad, grad_kernels, grad_in.T, grad_out


def solution(mesh):
    in_specs = (
        P(None, ("aa", "ba")),
        P(None, ("aa", "ba")),
        P(("aa", "ba"), None),
        P(None, ("aa", "ba")),
        P(),
        P(),
        P(),
        P(),
    )
    out_specs = (P(None, ("aa", "ba")), P(None, ("aa", "ba")), P(), P(), P())
    return jax.shard_map(local, mesh=mesh, in_specs=in_specs, out_specs=out_specs, check_vma=False)
```

```python
import functools

import jax
import jax.numpy as jnp
from jax import lax
from jax.experimental import pallas as pl
from jax.experimental.pallas import tpu as pltpu
from jax.sharding import PartitionSpec as P

F32 = jnp.float32
BF16 = jnp.bfloat16
NT = (((1,), (1,)), ((), ()))

DEVICES = 128
SLOTS = 128
PARTICLES = 4096
CHANNELS = 32
GZ = 64
CXD = 4
CYD = 32
PLANE = CYD * GZ
ROWS = 72
HALF = 40
TILE = 2 * GZ
TILES = PLANE // TILE
WIDE = PLANE + 4 * TILE
MID = PLANE + 2 * TILE
LOW = 16
HIGH = DEVICES // LOW


def params(mebibytes):
    return pltpu.CompilerParams(vmem_limit_bytes=mebibytes * 2**20)


def cost(macs, moved):
    return pl.CostEstimate(flops=2 * macs, bytes_accessed=moved, transcendentals=0)


def rows16(row):
    return jnp.broadcast_to(row, (16, row.shape[1]))


def silu_slope(value):
    sigma_value = jax.nn.sigmoid(value)
    return sigma_value * (1.0 + value * (1.0 - sigma_value))


def flipped(kernel):
    return jnp.transpose(kernel[::-1], (0, 2, 1))


def route_kernel(owner_ref, feat_ref, cot_ref, off_ref, out_ref, slot_ref, spread):
    block = 256
    owner_ids = lax.broadcasted_iota(jnp.int32, (DEVICES, block), 0)
    before = lax.broadcasted_iota(jnp.int32, (block, block + 128), 0)
    after = lax.broadcasted_iota(jnp.int32, (block, block + 128), 1)
    prefix = ((before < after) | (after >= block)).astype(F32).astype(BF16)
    base = jnp.zeros((DEVICES, 128), F32)
    ranks = []
    for number in range(PARTICLES // block):
        hot = (owner_ids == owner_ref[:, number * block : (number + 1) * block]).astype(F32)
        counted = jnp.dot(hot.astype(BF16), prefix, preferred_element_type=F32)
        earlier = counted[:, :block] + jnp.concatenate([base, base], axis=1)
        ranks.append(jnp.sum(hot * earlier, axis=0, keepdims=True))
        base = base + counted[:, block:]
    rank = jnp.concatenate(ranks, axis=1).astype(jnp.int32)
    owner = owner_ref[...]
    low = lax.rem(owner, LOW)
    slot = lax.div(owner, LOW) * SLOTS + rank
    slot_ref[...] = slot
    for group in range(LOW):
        mask = rows16((low == group).astype(F32)).astype(BF16)
        for field, source in enumerate((feat_ref, cot_ref)):
            for part in range(0, CHANNELS, 16):
                at = group * 2 * CHANNELS + field * CHANNELS + part
                spread[at : at + 16, :] = source[part : part + 16, :] * mask
    tail = LOW * 2 * CHANNELS
    offset = off_ref[...].astype(F32)
    nothing = jnp.zeros((1, PARTICLES), F32)
    offset = jnp.concatenate([offset, nothing, offset, nothing], axis=0)
    line = lax.div(lax.broadcasted_iota(jnp.int32, (8, PARTICLES), 0), 4)
    for group in range(0, LOW, 4):
        parts = [jnp.where(low == group + pair + line, offset, 0.0) for pair in (0, 2)]
        spread[tail + group * 4 : tail + group * 4 + 16, :] = jnp.concatenate(
            parts, axis=0
        ).astype(BF16)
    width = 256
    for step in range(HIGH * SLOTS // width):
        slot_ids = lax.broadcasted_iota(jnp.int32, (width, PARTICLES), 0) + step * width
        hot = (slot_ids == slot).astype(F32).astype(BF16)
        placed = lax.dot_general(spread[...], hot, NT, preferred_element_type=F32)
        for part in range(width // SLOTS):
            high = step * (width // SLOTS) + part
            lanes = slice(part * SLOTS, (part + 1) * SLOTS)
            for group in range(LOW):
                values = placed[group * 2 * CHANNELS : (group + 1) * 2 * CHANNELS, lanes]
                at = tail + group // 2 * 8
                where = placed[at : at + 8, lanes]
                if group % 2:
                    where = pltpu.roll(where, 4, 0)
                out_ref[high * LOW + group] = jnp.concatenate([values, where], axis=0).astype(BF16)


def route(owner, features, cotangent, offset):
    rows = LOW * (2 * CHANNELS + 4)
    return pl.pallas_call(
        route_kernel,
        out_shape=(
            jax.ShapeDtypeStruct((DEVICES, ROWS, SLOTS), BF16),
            jax.ShapeDtypeStruct((1, PARTICLES), jnp.int32),
        ),
        scratch_shapes=[pltpu.VMEM((rows, PARTICLES), BF16)],
        compiler_params=params(60),
        cost_estimate=cost(rows * PARTICLES * HIGH * SLOTS, 3 * 2**20),
    )(owner, features, cotangent, offset)


def network_kernel(feat_ref, cot_ref, in_ref, out_ref, in_t_ref, out_t_ref, local_ref, back_ref, grads_ref):
    step = pl.program_id(0)
    features = feat_ref[...]
    cotangent = cot_ref[...]
    hidden_pre = jnp.dot(in_ref[...], features, preferred_element_type=F32)
    hidden = jax.nn.silu(hidden_pre).astype(BF16)
    local_ref[...] = jnp.dot(out_ref[...], hidden, preferred_element_type=F32)
    hidden_back = jnp.dot(out_t_ref[...], cotangent, preferred_element_type=F32)
    pre_grad = (hidden_back * silu_slope(hidden_pre)).astype(BF16)
    back_ref[...] = jnp.dot(in_t_ref[...], pre_grad, preferred_element_type=F32)
    grad_in = lax.dot_general(features, pre_grad, NT, preferred_element_type=F32)
    grad_out = lax.dot_general(cotangent, hidden, NT, preferred_element_type=F32)
    both = jnp.concatenate([grad_in, grad_out], axis=0)

    @pl.when(step == 0)
    def first():
        grads_ref[...] = both

    @pl.when(step > 0)
    def later():
        grads_ref[...] += both


def network(features, cotangent, mlp_in, mlp_out):
    width = 1024
    hidden = mlp_in.shape[0]

    def whole(rows, columns):
        return pl.BlockSpec((rows, columns), lambda i: (0, 0))

    wide = pl.BlockSpec((CHANNELS, width), lambda i: (0, i))
    return pl.pallas_call(
        network_kernel,
        grid=(PARTICLES // width,),
        in_specs=[
            wide,
            wide,
            whole(hidden, CHANNELS),
            whole(CHANNELS, hidden),
            whole(CHANNELS, hidden),
            whole(hidden, CHANNELS),
        ],
        out_specs=(wide, wide, whole(2 * CHANNELS, hidden)),
        out_shape=(
            jax.ShapeDtypeStruct((CHANNELS, PARTICLES), F32),
            jax.ShapeDtypeStruct((CHANNELS, PARTICLES), F32),
            jax.ShapeDtypeStruct((2 * CHANNELS, hidden), F32),
        ),
        compiler_params=params(10),
        cost_estimate=cost(6 * 128 * 128 * PARTICLES, 2 * 2**20),
    )(features, cotangent, mlp_in, mlp_out, mlp_in.T, mlp_out.T)


def hat(position, at):
    return jnp.maximum(1.0 - jnp.abs(position - at), 0.0)


def places(offset):
    pos_x = offset[0:1] * float(CXD - 1)
    pos_y = jnp.broadcast_to(offset[1:2] * float(CYD - 1), (8, SLOTS))
    pos_z = offset[2:3] * float(GZ - 1)
    depth = lax.broadcasted_iota(jnp.int32, (GZ, SLOTS), 0).astype(F32)
    return pos_x, pos_y, hat(pos_z, depth)


def plane_weights(pos_y, weight_z, first, count):
    rows = []
    for y in [tile + half * TILES for tile in range(first, first + count) for half in range(2)]:
        weight_y = hat(pos_y, float(y))
        for part in range(GZ // 8):
            rows.append(weight_y * weight_z[part * 8 : part * 8 + 8])
    return jnp.concatenate(rows, axis=0).astype(BF16)


def scatter_kernel(blocks, in_ref, out_ref, head_x, tail_x, head_y, tail_y, total):
    step = pl.program_id(0)
    tiles = 2
    sources, placed = [], []
    for j in range(blocks):
        pos_x, pos_y, weight_z = places(in_ref[j, 64:72, :].astype(F32))
        placed.append((pos_y, weight_z))
        parts = []
        for field in range(2):
            values = in_ref[j, field * CHANNELS : (field + 1) * CHANNELS, :].astype(F32)
            for x in range(CXD):
                parts.append((values * hat(pos_x, float(x))).astype(BF16))
        sources.append(jnp.concatenate(parts, axis=0))
    source = jnp.concatenate(sources, axis=1)

    @pl.when(step == 0)
    def first():
        total[...] = jnp.zeros_like(total)

    for tile in range(0, TILES, tiles):
        weights = jnp.concatenate([plane_weights(*place, tile, tiles) for place in placed], axis=1)
        total[:, tile * TILE : (tile + tiles) * TILE] += lax.dot_general(
            source, weights, NT, preferred_element_type=F32
        )

    @pl.when(step == pl.num_programs(0) - 1)
    def last():
        rows = CXD * CHANNELS
        for field in range(2):
            cells = total[field * rows : (field + 1) * rows].astype(BF16)
            out_ref[field] = cells
            head_x[field] = cells[: rows // 2]
            tail_x[field] = cells[rows // 2 :]
            head_y[field] = cells[:, : 2 * TILE]
            tail_y[field] = cells[:, PLANE - 2 * TILE :]


def scatter(arrived):
    blocks = 32
    rows = CXD * CHANNELS
    shapes = [(2, rows, PLANE)] + [(2, rows // 2, PLANE)] * 2 + [(2, rows, 2 * TILE)] * 2
    return pl.pallas_call(
        functools.partial(scatter_kernel, blocks),
        grid=(DEVICES // blocks,),
        in_specs=[pl.BlockSpec((blocks, ROWS, SLOTS), lambda i: (i, 0, 0))],
        out_specs=[pl.BlockSpec(shape, lambda i: (0, 0, 0)) for shape in shapes],
        out_shape=[jax.ShapeDtypeStruct(shape, BF16) for shape in shapes],
        scratch_shapes=[pltpu.VMEM((2 * rows, PLANE), F32)],
        compiler_params=params(20),
        cost_estimate=cost(256 * PLANE * DEVICES * SLOTS, 4 * 2**20),
    )(arrived)


def gather_kernel(blocks, *refs):
    in_ref, grid_ref, out_ref = refs[0], refs[1], refs[-1]
    tiles = 2
    placed = [places(in_ref[j].astype(F32)) for j in range(blocks)]
    total = None
    for tile in range(0, TILES, tiles):
        weights = jnp.concatenate(
            [plane_weights(pos_y, weight_z, tile, tiles) for _, pos_y, weight_z in placed], axis=1
        )
        product = jnp.dot(
            grid_ref[:, tile * TILE : (tile + tiles) * TILE], weights, preferred_element_type=F32
        )
        total = product if total is None else total + product
    for j in range(blocks):
        summed = None
        for x in range(CXD):
            part = total[x * CHANNELS : (x + 1) * CHANNELS, j * SLOTS : (j + 1) * SLOTS]
            part = part * hat(placed[j][0], float(x))
            summed = part if summed is None else summed + part
        if len(refs) == 3:
            out_ref[j, :CHANNELS, :] = summed.astype(BF16)
        else:
            sums = refs[2][j // 2]
            high = sums.astype(BF16).astype(F32)
            rest = sums - high
            upper = lax.broadcasted_iota(jnp.int32, (8, SLOTS), 0) < 4
            if j % 2:
                both = jnp.where(upper, pltpu.roll(high, 4, 0), rest)
            else:
                both = jnp.where(upper, high, pltpu.roll(rest, 4, 0))
            out_ref[j] = jnp.concatenate([summed, both], axis=0).astype(BF16)


def gather(arrived, grids, *parts):
    blocks = 16
    rows = HALF if parts else CHANNELS
    return pl.pallas_call(
        functools.partial(gather_kernel, blocks),
        grid=(DEVICES // blocks,),
        in_specs=[
            pl.BlockSpec((blocks, 8, SLOTS), lambda i: (i, 8, 0)),
            pl.BlockSpec((CXD * CHANNELS, PLANE), lambda i: (0, 0)),
        ]
        + [pl.BlockSpec((blocks // 2, 8, SLOTS), lambda i: (i, 0, 0)) for _ in parts],
        out_specs=pl.BlockSpec((blocks, rows, SLOTS), lambda i: (i, 0, 0)),
        out_shape=jax.ShapeDtypeStruct((DEVICES, HALF, SLOTS), BF16),
        compiler_params=params(12),
        cost_estimate=cost(128 * PLANE * DEVICES * SLOTS, 3 * 2**20),
    )(arrived, grids, *parts)


def attach_kernel(parts_ref, held_ref, out_ref):
    del held_ref
    total = jnp.sum(parts_ref[...].astype(F32), axis=0)
    total = total + pltpu.roll(total, 4, 0)
    high = total.astype(BF16).astype(F32)
    upper = lax.broadcasted_iota(jnp.int32, (8, SLOTS), 0) < 4
    both = jnp.where(upper, high, total - high).astype(BF16)
    out_ref[...] = jnp.broadcast_to(both[None], out_ref.shape)


def attach(returned, payload):
    rows = pl.BlockSpec((DEVICES, 8, SLOTS), lambda i: (0, CHANNELS // 8, 0))
    return pl.pallas_call(
        attach_kernel,
        grid=(1,),
        in_specs=[rows, pl.BlockSpec(memory_space=pl.ANY)],
        out_specs=rows,
        out_shape=jax.ShapeDtypeStruct((DEVICES, HALF, SLOTS), BF16),
        input_output_aliases={1: 0},
        compiler_params=params(4),
        cost_estimate=cost(10**5, 2**19),
    )(returned, payload)


def moved(piece, axis, step):
    count = lax.axis_size(axis)
    pairs = [(i, i + step) for i in range(count) if 0 <= i + step < count]
    return lax.ppermute(piece, axis, pairs)


def border_kernel(x_low, x_high, head_y, tail_y, head_ref, tail_ref):
    edge = 2 * TILE
    for field in range(2):
        for own, at, out in ((head_y, 0, head_ref), (tail_y, PLANE - edge, tail_ref)):
            parts = [x_low[field, :, at : at + edge], own[field], x_high[field, :, at : at + edge]]
            out[field] = jnp.concatenate(parts, axis=0)


def borders(x_low, x_high, head_y, tail_y):
    shape = jax.ShapeDtypeStruct((2, 8 * CHANNELS, 2 * TILE), BF16)
    return pl.pallas_call(
        border_kernel,
        out_shape=[shape, shape],
        compiler_params=params(8),
        cost_estimate=cost(10**6, 2 * 2**20),
    )(x_low, x_high, head_y, tail_y)


def shifted(value, out):
    rows, lanes = value.shape
    depth = lax.rem(lax.broadcasted_iota(jnp.int32, (1, lanes), 1), GZ)
    wide = value.astype(F32)
    before = jnp.where(depth == 0, 0.0, pltpu.roll(wide, 1, 1))
    after = jnp.where(depth == GZ - 1, 0.0, pltpu.roll(wide, lanes - 1, 1))
    out[:rows, :] = before.astype(BF16)
    out[rows : 2 * rows, :] = value
    out[2 * rows :, :] = after.astype(BF16)


def convolved(weights, source, lanes):
    total = None
    for step in range(3):
        product = jnp.dot(
            weights[step],
            source[:, step * TILE : step * TILE + lanes],
            preferred_element_type=F32,
        )
        total = product if total is None else total + product
    return total


def conv_kernel(
    own, x_low, x_high, y_low, y_high, w_one, w_back, w_two, small_ref,
    out_ref, pre_ref, grads_ref, zeros, backs, acts, reduced,
):
    spot_a = lax.axis_index("aa")
    spot_b = lax.axis_index("ba")

    edge = 2 * TILE
    half = lax.rem(lax.div(lax.broadcasted_iota(jnp.int32, (1, edge), 1), GZ), 2)
    for field, out in enumerate((zeros, backs)):
        planes = jnp.concatenate([x_low[field], own[field], x_high[field]], axis=0)
        first, last = planes[:, :edge].astype(F32), planes[:, PLANE - edge :].astype(F32)
        below = jnp.where(half == 1, y_low[field].astype(F32), last)
        above = jnp.where(half == 0, y_high[field].astype(F32), first)
        below, above = [
            jnp.concatenate(
                [pltpu.roll(side[:, at : at + TILE], GZ, 1) for at in (0, TILE)], axis=1
            ).astype(BF16)
            for side in (below, above)
        ]
        shifted(jnp.concatenate([below, planes, above], axis=1), out)

    pre_one = convolved(w_one, zeros, MID)
    act_back = convolved(w_back, backs, MID)
    plane = lax.div(lax.broadcasted_iota(jnp.int32, (6 * CHANNELS, 1), 0), CHANNELS)
    line = lax.div(lax.broadcasted_iota(jnp.int32, (1, MID), 1), GZ)
    outside_x = ((plane == 0) & (spot_b == 0)) | (
        (plane == CXD + 1) & (spot_b == lax.axis_size("ba") - 1)
    )
    outside_y = ((line == 0) & (spot_a == 0)) | (
        (line == MID // GZ - 1) & (spot_a == lax.axis_size("aa") - 1)
    )
    inside = jnp.where(outside_x, 0.0, 1.0) * jnp.where(outside_y, 0.0, 1.0)
    sigma = jax.nn.sigmoid(pre_one)
    shifted((pre_one * sigma * inside).astype(BF16), acts)
    slope = sigma * (1.0 + pre_one * (1.0 - sigma))
    pre_back = (act_back * slope * inside).astype(BF16)
    pre_ref[...] = pre_back
    rows = 6 * CHANNELS
    own_rows = CXD * CHANNELS
    grid_one = own[0].astype(F32) + convolved(w_two, acts, PLANE)
    out_ref[...] = grid_one.astype(BF16)

    upstream = (pre_back[CHANNELS : CHANNELS + own_rows, TILE : TILE + PLANE], own[1])
    row_plane = lax.div(lax.broadcasted_iota(jnp.int32, (own_rows, rows), 0), CHANNELS)
    col_plane = lax.div(lax.broadcasted_iota(jnp.int32, (own_rows, rows), 1), CHANNELS)
    for conv in range(2):
        for step_y in range(3):
            for step_z in range(3):
                if conv == 0:
                    start = step_z * 8 * CHANNELS + CHANNELS
                    at = (step_y + 1) * TILE
                    field = zeros[start : start + rows, at : at + PLANE]
                else:
                    at = step_y * TILE
                    field = acts[step_z * rows : (step_z + 1) * rows, at : at + PLANE]
                product = lax.dot_general(upstream[conv], field, NT, preferred_element_type=F32)
                for step_x in range(3):
                    kept = jnp.where(col_plane == row_plane + step_x, product, 0.0)
                    folded = kept[:CHANNELS]
                    for x in range(1, CXD):
                        folded = folded + kept[x * CHANNELS : (x + 1) * CHANNELS]
                    at = (conv * 27 + step_x * 9 + step_y * 3 + step_z) * CHANNELS
                    reduced[at : at + CHANNELS, :] = folded
    quarter = 2 * 27 * CHANNELS // 4
    total = None
    for part in range(4):
        source = lax.broadcasted_iota(jnp.int32, (rows, 128), 0)
        target = lax.broadcasted_iota(jnp.int32, (rows, 128), 1)
        chosen = (target == lax.rem(source, CHANNELS) + part * CHANNELS).astype(F32)
        product = jnp.dot(
            reduced[part * quarter : (part + 1) * quarter, :],
            chosen,
            preferred_element_type=F32,
            precision=lax.Precision.HIGHEST,
        )
        total = product if total is None else total + product
    small = small_ref[...]
    filler = jnp.zeros((4 * DEVICES - quarter - small.shape[0], SLOTS), F32)
    grads_ref[:quarter] = total
    grads_ref[quarter:] = jnp.concatenate([small, filler], axis=0)


def band(kernel, planes):
    taps = kernel.reshape(3, 3, 3, CHANNELS, CHANNELS)
    taps = jnp.transpose(taps, (1, 3, 2, 0, 4))
    taps = jnp.pad(taps, ((0, 0), (0, 0), (0, 0), (0, planes - 1), (0, 0)))
    return taps.reshape(3, CHANNELS, 3 * (planes + 2) * CHANNELS)


def toeplitz_kernel(*refs):
    for band_ref, out_ref in zip(refs[:4], refs[4:]):
        for step in range(3):
            first = band_ref[step].astype(F32)
            for x in range(out_ref.shape[1] // CHANNELS):
                moved = first if x == 0 else pltpu.roll(first, x * CHANNELS, 1)
                out_ref[step, x * CHANNELS : (x + 1) * CHANNELS, :] = moved.astype(BF16)


def toeplitz(kernel_one, kernel_two):
    bands = (
        band(kernel_one, 6),
        band(flipped(kernel_two), 6),
        band(kernel_two, 4),
        band(flipped(kernel_one), 4),
    )
    return pl.pallas_call(
        toeplitz_kernel,
        out_shape=[
            jax.ShapeDtypeStruct((3, planes * CHANNELS, 3 * (planes + 2) * CHANNELS), BF16)
            for planes in (6, 6, 4, 4)
        ],
        compiler_params=params(10),
        cost_estimate=cost(10**7, 4 * 2**20),
    )(*bands)


def conv_block(grids, edges, weights, small):
    rows_one = 3 * 8 * CHANNELS
    rows_two = 3 * 6 * CHANNELS
    shape = jax.ShapeDtypeStruct((CXD * CHANNELS, PLANE), BF16)
    return pl.pallas_call(
        conv_kernel,
        out_shape=(
            shape,
            jax.ShapeDtypeStruct((6 * CHANNELS, MID), BF16),
            jax.ShapeDtypeStruct((4 * DEVICES, SLOTS), F32),
        ),
        scratch_shapes=[
            pltpu.VMEM((rows_one, WIDE), BF16),
            pltpu.VMEM((rows_one, WIDE), BF16),
            pltpu.VMEM((rows_two, MID), BF16),
            pltpu.VMEM((2 * 27 * CHANNELS, 6 * CHANNELS), F32),
        ],
        compiler_params=params(28),
        cost_estimate=cost(6 * 10**9, 8 * 2**20),
    )(grids, *edges, *weights[:3], small)


def last_kernel(own, pre_ref, w_last, out_ref, pres):
    shifted(pre_ref[...], pres)
    out_ref[...] = (own[0].astype(F32) + convolved(w_last, pres, PLANE)).astype(BF16)


def last_conv(grids, pre_back, weight):
    rows = CXD * CHANNELS
    return pl.pallas_call(
        last_kernel,
        grid=(1,),
        in_specs=[
            pl.BlockSpec((1, rows, PLANE), lambda i: (1, 0, 0)),
            pl.BlockSpec(pre_back.shape, lambda i: (0, 0)),
            pl.BlockSpec(weight.shape, lambda i: (0, 0, 0)),
        ],
        out_specs=pl.BlockSpec((rows, PLANE), lambda i: (0, 0)),
        out_shape=jax.ShapeDtypeStruct((rows, PLANE), BF16),
        scratch_shapes=[pltpu.VMEM((3 * 6 * CHANNELS, MID), BF16)],
        compiler_params=params(10),
        cost_estimate=cost(10**9, 2 * 2**20),
    )(grids, pre_back, weight)


def unroute_kernel(ret_ref, slot_ref, owner_ref, local_ref, out_ref, *refs):
    rows = CHANNELS
    table = refs[-1]
    for high in range(HIGH):
        for low in range(LOW):
            table[low * rows : (low + 1) * rows, high * SLOTS : (high + 1) * SLOTS] = ret_ref[
                high * LOW + low, :rows, :
            ]
    width = 512
    for step in range(PARTICLES // width):
        lanes = slice(step * width, (step + 1) * width)
        slot_ids = lax.broadcasted_iota(jnp.int32, (HIGH * SLOTS, width), 0)
        hot = (slot_ids == slot_ref[:, lanes]).astype(F32).astype(BF16)
        found = jnp.dot(table[...], hot, preferred_element_type=F32)
        low = lax.rem(owner_ref[:, lanes], LOW)
        mine = None
        for group in range(LOW):
            part = jnp.where(low == group, found[group * rows : (group + 1) * rows], 0.0)
            mine = part if mine is None else mine + part
        out_ref[:, lanes] = (mine + local_ref[:, lanes]).astype(BF16)
    if len(refs) == 1:
        return

    kernels_ref, in_ref, mlp_ref = refs[:3]
    halves = ret_ref[:, rows:, :].astype(F32)
    summed = (halves + pltpu.roll(halves, 4, 1)).reshape(DEVICES // 2, 2, 8, SLOTS)
    upper = lax.broadcasted_iota(jnp.int32, (DEVICES // 2, 8, SLOTS), 1) < 4
    summed = jnp.where(upper, summed[:, 0], summed[:, 1]).reshape(4 * DEVICES, SLOTS)
    quarter = 2 * 27 * CHANNELS // 4
    for part in range(4):
        turned = summed[:quarter]
        if part:
            turned = pltpu.roll(turned, 128 - part * CHANNELS, 1)
        kernels_ref[part * quarter : (part + 1) * quarter, :] = turned[:, :CHANNELS]
    in_ref[...] = summed[quarter : quarter + CHANNELS]
    mlp_ref[...] = summed[quarter + CHANNELS : quarter + 2 * CHANNELS]


def unroute(returned, slot, owner, addend, sums):
    shapes = [jax.ShapeDtypeStruct((CHANNELS, PARTICLES), BF16)]
    if sums:
        shapes += [
            jax.ShapeDtypeStruct((2 * 27 * CHANNELS, CHANNELS), F32),
            jax.ShapeDtypeStruct((CHANNELS, 128), F32),
            jax.ShapeDtypeStruct((CHANNELS, 128), F32),
        ]
    return pl.pallas_call(
        unroute_kernel,
        out_shape=shapes,
        scratch_shapes=[pltpu.VMEM((LOW * CHANNELS, HIGH * SLOTS), BF16)],
        compiler_params=params(14),
        cost_estimate=cost(512 * 1024 * PARTICLES, 3 * 2**20),
    )(returned, slot, owner, addend)


def exchanged(blocks):
    return lax.all_to_all(blocks, ("aa", "ba"), split_axis=0, concat_axis=0, tiled=True)


def local(features, cotangent, owner, offset, kernel_one, kernel_two, mlp_in, mlp_out):
    owner = owner.reshape(1, PARTICLES)
    outgoing, slot = route(owner, features, cotangent, offset)
    arrived = exchanged(outgoing)
    local_out, local_back, small = network(features, cotangent, mlp_in, mlp_out)
    weights = toeplitz(kernel_one, kernel_two)
    arrived, weights, small = lax.optimization_barrier((arrived, weights, small))
    grids, head_x, tail_x, head_y, tail_y = scatter(arrived)
    x_low, x_high = moved(tail_x, "ba", 1), moved(head_x, "ba", -1)
    border_head, border_tail = borders(x_low, x_high, head_y, tail_y)
    y_low, y_high = moved(border_tail, "aa", 1), moved(border_head, "aa", -1)
    edges = (x_low, x_high, y_low, y_high)
    grid_one, pre_back, parts = conv_block(grids, edges, weights, small)
    first = exchanged(gather(arrived, grid_one, parts.reshape(DEVICES // 2, 8, SLOTS)))
    back_zero = last_conv(grids, pre_back, weights[3])
    second = exchanged(attach(first, gather(arrived, back_zero)))
    (particle_out,) = unroute(first, slot, owner, local_out, False)
    feat_grad, grad_kernels, grad_in, grad_out = unroute(second, slot, owner, local_back, True)
    grad_kernels = grad_kernels.reshape(2, 27, CHANNELS, CHANNELS)
    return particle_out, feat_grad, grad_kernels, grad_in.T, grad_out


def solution(mesh):
    in_specs = (
        P(None, ("aa", "ba")),
        P(None, ("aa", "ba")),
        P(("aa", "ba"), None),
        P(None, ("aa", "ba")),
        P(),
        P(),
        P(),
        P(),
    )
    out_specs = (P(None, ("aa", "ba")), P(None, ("aa", "ba")), P(), P(), P())
    return jax.shard_map(local, mesh=mesh, in_specs=in_specs, out_specs=out_specs, check_vma=False)
```

```python
import functools

import jax
import jax.numpy as jnp
from jax import lax
from jax.experimental import pallas as pl
from jax.experimental.pallas import tpu as pltpu
from jax.sharding import PartitionSpec as P

F32 = jnp.float32
BF16 = jnp.bfloat16
NT = (((1,), (1,)), ((), ()))

DEVICES = 128
SLOTS = 128
PARTICLES = 4096
CHANNELS = 32
GZ = 64
CXD = 4
CYD = 32
PLANE = CYD * GZ
ROWS = 72
HALF = 40
TILE = 2 * GZ
TILES = PLANE // TILE
WIDE = PLANE + 4 * TILE
MID = PLANE + 2 * TILE
LOW = 16
HIGH = DEVICES // LOW


def params(mebibytes):
    return pltpu.CompilerParams(vmem_limit_bytes=mebibytes * 2**20)


def cost(macs, moved):
    return pl.CostEstimate(flops=2 * macs, bytes_accessed=moved, transcendentals=0)


def rows16(row):
    return jnp.broadcast_to(row, (16, row.shape[1]))


def silu_slope(value):
    sigma_value = jax.nn.sigmoid(value)
    return sigma_value * (1.0 + value * (1.0 - sigma_value))


def flipped(kernel):
    return jnp.transpose(kernel[::-1], (0, 2, 1))


def route_kernel(owner_ref, feat_ref, cot_ref, off_ref, out_ref, slot_ref, spread):
    block = 256
    owner_ids = lax.broadcasted_iota(jnp.int32, (DEVICES, block), 0)
    before = lax.broadcasted_iota(jnp.int32, (block, block + 128), 0)
    after = lax.broadcasted_iota(jnp.int32, (block, block + 128), 1)
    prefix = ((before < after) | (after >= block)).astype(F32).astype(BF16)
    base = jnp.zeros((DEVICES, 128), F32)
    ranks = []
    for number in range(PARTICLES // block):
        hot = (owner_ids == owner_ref[:, number * block : (number + 1) * block]).astype(F32)
        counted = jnp.dot(hot.astype(BF16), prefix, preferred_element_type=F32)
        earlier = counted[:, :block] + jnp.concatenate([base, base], axis=1)
        ranks.append(jnp.sum(hot * earlier, axis=0, keepdims=True))
        base = base + counted[:, block:]
    rank = jnp.concatenate(ranks, axis=1).astype(jnp.int32)
    owner = owner_ref[...]
    low = lax.rem(owner, LOW)
    slot = lax.div(owner, LOW) * SLOTS + rank
    slot_ref[...] = slot
    for group in range(LOW):
        mask = rows16((low == group).astype(F32)).astype(BF16)
        for field, source in enumerate((feat_ref, cot_ref)):
            for part in range(0, CHANNELS, 16):
                at = group * 2 * CHANNELS + field * CHANNELS + part
                spread[at : at + 16, :] = source[part : part + 16, :] * mask
    tail = LOW * 2 * CHANNELS
    offset = off_ref[...].astype(F32)
    nothing = jnp.zeros((1, PARTICLES), F32)
    offset = jnp.concatenate([offset, nothing, offset, nothing], axis=0)
    line = lax.div(lax.broadcasted_iota(jnp.int32, (8, PARTICLES), 0), 4)
    for group in range(0, LOW, 4):
        parts = [jnp.where(low == group + pair + line, offset, 0.0) for pair in (0, 2)]
        spread[tail + group * 4 : tail + group * 4 + 16, :] = jnp.concatenate(
            parts, axis=0
        ).astype(BF16)
    width = 256
    for step in range(HIGH * SLOTS // width):
        slot_ids = lax.broadcasted_iota(jnp.int32, (width, PARTICLES), 0) + step * width
        hot = (slot_ids == slot).astype(F32).astype(BF16)
        placed = lax.dot_general(spread[...], hot, NT, preferred_element_type=F32)
        for part in range(width // SLOTS):
            high = step * (width // SLOTS) + part
            lanes = slice(part * SLOTS, (part + 1) * SLOTS)
            for group in range(LOW):
                values = placed[group * 2 * CHANNELS : (group + 1) * 2 * CHANNELS, lanes]
                at = tail + group // 2 * 8
                where = placed[at : at + 8, lanes]
                if group % 2:
                    where = pltpu.roll(where, 4, 0)
                out_ref[high * LOW + group] = jnp.concatenate([values, where], axis=0).astype(BF16)


def route(owner, features, cotangent, offset):
    rows = LOW * (2 * CHANNELS + 4)
    return pl.pallas_call(
        route_kernel,
        out_shape=(
            jax.ShapeDtypeStruct((DEVICES, ROWS, SLOTS), BF16),
            jax.ShapeDtypeStruct((1, PARTICLES), jnp.int32),
        ),
        scratch_shapes=[pltpu.VMEM((rows, PARTICLES), BF16)],
        compiler_params=params(60),
        cost_estimate=cost(rows * PARTICLES * HIGH * SLOTS, 3 * 2**20),
    )(owner, features, cotangent, offset)


def network_kernel(feat_ref, cot_ref, in_ref, out_ref, in_t_ref, out_t_ref, local_ref, back_ref, grads_ref):
    step = pl.program_id(0)
    features = feat_ref[...]
    cotangent = cot_ref[...]
    hidden_pre = jnp.dot(in_ref[...], features, preferred_element_type=F32)
    hidden = jax.nn.silu(hidden_pre).astype(BF16)
    local_ref[...] = jnp.dot(out_ref[...], hidden, preferred_element_type=F32)
    hidden_back = jnp.dot(out_t_ref[...], cotangent, preferred_element_type=F32)
    pre_grad = (hidden_back * silu_slope(hidden_pre)).astype(BF16)
    back_ref[...] = jnp.dot(in_t_ref[...], pre_grad, preferred_element_type=F32)
    grad_in = lax.dot_general(features, pre_grad, NT, preferred_element_type=F32)
    grad_out = lax.dot_general(cotangent, hidden, NT, preferred_element_type=F32)
    both = jnp.concatenate([grad_in, grad_out], axis=0)

    @pl.when(step == 0)
    def first():
        grads_ref[...] = both

    @pl.when(step > 0)
    def later():
        grads_ref[...] += both


def network(features, cotangent, mlp_in, mlp_out):
    width = 1024
    hidden = mlp_in.shape[0]

    def whole(rows, columns):
        return pl.BlockSpec((rows, columns), lambda i: (0, 0))

    wide = pl.BlockSpec((CHANNELS, width), lambda i: (0, i))
    return pl.pallas_call(
        network_kernel,
        grid=(PARTICLES // width,),
        in_specs=[
            wide,
            wide,
            whole(hidden, CHANNELS),
            whole(CHANNELS, hidden),
            whole(CHANNELS, hidden),
            whole(hidden, CHANNELS),
        ],
        out_specs=(wide, wide, whole(2 * CHANNELS, hidden)),
        out_shape=(
            jax.ShapeDtypeStruct((CHANNELS, PARTICLES), F32),
            jax.ShapeDtypeStruct((CHANNELS, PARTICLES), F32),
            jax.ShapeDtypeStruct((2 * CHANNELS, hidden), F32),
        ),
        compiler_params=params(10),
        cost_estimate=cost(6 * 128 * 128 * PARTICLES, 2 * 2**20),
    )(features, cotangent, mlp_in, mlp_out, mlp_in.T, mlp_out.T)


def hat(position, at):
    return jnp.maximum(1.0 - jnp.abs(position - at), 0.0)


def places(offset):
    pos_x = offset[0:1] * float(CXD - 1)
    pos_y = jnp.broadcast_to(offset[1:2] * float(CYD - 1), (8, SLOTS))
    pos_z = offset[2:3] * float(GZ - 1)
    depth = lax.broadcasted_iota(jnp.int32, (GZ, SLOTS), 0).astype(F32)
    return pos_x, pos_y, hat(pos_z, depth)


def plane_weights(pos_y, weight_z, first, count):
    rows = []
    for y in [tile + half * TILES for tile in range(first, first + count) for half in range(2)]:
        weight_y = hat(pos_y, float(y))
        for part in range(GZ // 8):
            rows.append(weight_y * weight_z[part * 8 : part * 8 + 8])
    return jnp.concatenate(rows, axis=0).astype(BF16)


def scatter_kernel(blocks, in_ref, out_ref, head_x, tail_x, head_y, tail_y, total):
    step = pl.program_id(0)
    tiles = 2
    sources, placed = [], []
    for j in range(blocks):
        pos_x, pos_y, weight_z = places(in_ref[j, 64:72, :].astype(F32))
        placed.append((pos_y, weight_z))
        parts = []
        for field in range(2):
            values = in_ref[j, field * CHANNELS : (field + 1) * CHANNELS, :].astype(F32)
            for x in range(CXD):
                parts.append((values * hat(pos_x, float(x))).astype(BF16))
        sources.append(jnp.concatenate(parts, axis=0))
    source = jnp.concatenate(sources, axis=1)

    @pl.when(step == 0)
    def first():
        total[...] = jnp.zeros_like(total)

    for tile in range(0, TILES, tiles):
        weights = jnp.concatenate([plane_weights(*place, tile, tiles) for place in placed], axis=1)
        total[:, tile * TILE : (tile + tiles) * TILE] += lax.dot_general(
            source, weights, NT, preferred_element_type=F32
        )

    @pl.when(step == pl.num_programs(0) - 1)
    def last():
        rows = CXD * CHANNELS
        for field in range(2):
            cells = total[field * rows : (field + 1) * rows].astype(BF16)
            out_ref[field] = cells
            head_x[field] = cells[: rows // 2]
            tail_x[field] = cells[rows // 2 :]
            head_y[field] = cells[:, : 2 * TILE]
            tail_y[field] = cells[:, PLANE - 2 * TILE :]


def scatter(arrived):
    blocks = 32
    rows = CXD * CHANNELS
    shapes = [(2, rows, PLANE)] + [(2, rows // 2, PLANE)] * 2 + [(2, rows, 2 * TILE)] * 2
    return pl.pallas_call(
        functools.partial(scatter_kernel, blocks),
        grid=(DEVICES // blocks,),
        in_specs=[pl.BlockSpec((blocks, ROWS, SLOTS), lambda i: (i, 0, 0))],
        out_specs=[pl.BlockSpec(shape, lambda i: (0, 0, 0)) for shape in shapes],
        out_shape=[jax.ShapeDtypeStruct(shape, BF16) for shape in shapes],
        scratch_shapes=[pltpu.VMEM((2 * rows, PLANE), F32)],
        compiler_params=params(20),
        cost_estimate=cost(256 * PLANE * DEVICES * SLOTS, 4 * 2**20),
    )(arrived)


def gather_kernel(blocks, *refs):
    in_ref, grid_ref, out_ref = refs[0], refs[1], refs[-1]
    tiles = 2
    placed = [places(in_ref[j].astype(F32)) for j in range(blocks)]
    total = None
    for tile in range(0, TILES, tiles):
        weights = jnp.concatenate(
            [plane_weights(pos_y, weight_z, tile, tiles) for _, pos_y, weight_z in placed], axis=1
        )
        product = jnp.dot(
            grid_ref[:, tile * TILE : (tile + tiles) * TILE], weights, preferred_element_type=F32
        )
        total = product if total is None else total + product
    for j in range(blocks):
        summed = None
        for x in range(CXD):
            part = total[x * CHANNELS : (x + 1) * CHANNELS, j * SLOTS : (j + 1) * SLOTS]
            part = part * hat(placed[j][0], float(x))
            summed = part if summed is None else summed + part
        if len(refs) == 3:
            out_ref[j, :CHANNELS, :] = summed.astype(BF16)
        else:
            sums = refs[2][j // 2]
            high = sums.astype(BF16).astype(F32)
            rest = sums - high
            upper = lax.broadcasted_iota(jnp.int32, (8, SLOTS), 0) < 4
            if j % 2:
                both = jnp.where(upper, pltpu.roll(high, 4, 0), rest)
            else:
                both = jnp.where(upper, high, pltpu.roll(rest, 4, 0))
            out_ref[j] = jnp.concatenate([summed, both], axis=0).astype(BF16)


def gather(arrived, grids, *parts):
    blocks = 16
    rows = HALF if parts else CHANNELS
    return pl.pallas_call(
        functools.partial(gather_kernel, blocks),
        grid=(DEVICES // blocks,),
        in_specs=[
            pl.BlockSpec((blocks, 8, SLOTS), lambda i: (i, 8, 0)),
            pl.BlockSpec((CXD * CHANNELS, PLANE), lambda i: (0, 0)),
        ]
        + [pl.BlockSpec((blocks // 2, 8, SLOTS), lambda i: (i, 0, 0)) for _ in parts],
        out_specs=pl.BlockSpec((blocks, rows, SLOTS), lambda i: (i, 0, 0)),
        out_shape=jax.ShapeDtypeStruct((DEVICES, HALF, SLOTS), BF16),
        compiler_params=params(12),
        cost_estimate=cost(128 * PLANE * DEVICES * SLOTS, 3 * 2**20),
    )(arrived, grids, *parts)


def attach_kernel(parts_ref, held_ref, out_ref):
    del held_ref
    total = jnp.sum(parts_ref[...].astype(F32), axis=0)
    total = total + pltpu.roll(total, 4, 0)
    high = total.astype(BF16).astype(F32)
    upper = lax.broadcasted_iota(jnp.int32, (8, SLOTS), 0) < 4
    both = jnp.where(upper, high, total - high).astype(BF16)
    out_ref[...] = jnp.broadcast_to(both[None], out_ref.shape)


def attach(returned, payload):
    rows = pl.BlockSpec((DEVICES, 8, SLOTS), lambda i: (0, CHANNELS // 8, 0))
    return pl.pallas_call(
        attach_kernel,
        grid=(1,),
        in_specs=[rows, pl.BlockSpec(memory_space=pl.ANY)],
        out_specs=rows,
        out_shape=jax.ShapeDtypeStruct((DEVICES, HALF, SLOTS), BF16),
        input_output_aliases={1: 0},
        compiler_params=params(4),
        cost_estimate=cost(10**5, 2**19),
    )(returned, payload)


def moved(piece, axis, step):
    count = lax.axis_size(axis)
    pairs = [(i, i + step) for i in range(count) if 0 <= i + step < count]
    return lax.ppermute(piece, axis, pairs)


def border_kernel(x_low, x_high, head_y, tail_y, head_ref, tail_ref):
    edge = 2 * TILE
    for field in range(2):
        for own, at, out in ((head_y, 0, head_ref), (tail_y, PLANE - edge, tail_ref)):
            parts = [x_low[field, :, at : at + edge], own[field], x_high[field, :, at : at + edge]]
            out[field] = jnp.concatenate(parts, axis=0)


def borders(x_low, x_high, head_y, tail_y):
    shape = jax.ShapeDtypeStruct((2, 8 * CHANNELS, 2 * TILE), BF16)
    return pl.pallas_call(
        border_kernel,
        out_shape=[shape, shape],
        compiler_params=params(8),
        cost_estimate=cost(10**6, 2 * 2**20),
    )(x_low, x_high, head_y, tail_y)


def shifted(value, out):
    rows, lanes = value.shape
    depth = lax.rem(lax.broadcasted_iota(jnp.int32, (1, lanes), 1), GZ)
    wide = value.astype(F32)
    before = jnp.where(depth == 0, 0.0, pltpu.roll(wide, 1, 1))
    after = jnp.where(depth == GZ - 1, 0.0, pltpu.roll(wide, lanes - 1, 1))
    out[:rows, :] = before.astype(BF16)
    out[rows : 2 * rows, :] = value
    out[2 * rows : 3 * rows, :] = after.astype(BF16)


def convolved(weights, source, lanes):
    total = None
    for step in range(3):
        product = jnp.dot(
            weights[step],
            source[: weights.shape[2], step * TILE : step * TILE + lanes],
            preferred_element_type=F32,
        )
        total = product if total is None else total + product
    return total


def conv_kernel(
    own, x_low, x_high, y_low, y_high, w_one, w_back, w_two, small_ref,
    out_ref, pre_ref, grads_ref, zeros, backs, acts, reduced,
):
    spot_a = lax.axis_index("aa")
    spot_b = lax.axis_index("ba")

    edge = 2 * TILE
    half = lax.rem(lax.div(lax.broadcasted_iota(jnp.int32, (1, edge), 1), GZ), 2)
    for field, out in enumerate((zeros, backs)):
        planes = jnp.concatenate([x_low[field], own[field], x_high[field]], axis=0)
        first, last = planes[:, :edge].astype(F32), planes[:, PLANE - edge :].astype(F32)
        below = jnp.where(half == 1, y_low[field].astype(F32), last)
        above = jnp.where(half == 0, y_high[field].astype(F32), first)
        below, above = [
            jnp.concatenate(
                [pltpu.roll(side[:, at : at + TILE], GZ, 1) for at in (0, TILE)], axis=1
            ).astype(BF16)
            for side in (below, above)
        ]
        shifted(jnp.concatenate([below, planes, above], axis=1), out)

    pre_one = convolved(w_one, zeros, MID)
    act_back = convolved(w_back, backs, MID)
    plane = lax.div(lax.broadcasted_iota(jnp.int32, (6 * CHANNELS, 1), 0), CHANNELS)
    line = lax.div(lax.broadcasted_iota(jnp.int32, (1, MID), 1), GZ)
    outside_x = ((plane == 0) & (spot_b == 0)) | (
        (plane == CXD + 1) & (spot_b == lax.axis_size("ba") - 1)
    )
    outside_y = ((line == 0) & (spot_a == 0)) | (
        (line == MID // GZ - 1) & (spot_a == lax.axis_size("aa") - 1)
    )
    inside = jnp.where(outside_x, 0.0, 1.0) * jnp.where(outside_y, 0.0, 1.0)
    sigma = jax.nn.sigmoid(pre_one)
    shifted((pre_one * sigma * inside).astype(BF16), acts)
    slope = sigma * (1.0 + pre_one * (1.0 - sigma))
    pre_back = (act_back * slope * inside).astype(BF16)
    pre_ref[...] = pre_back
    rows = 6 * CHANNELS
    own_rows = CXD * CHANNELS
    grid_one = own[0].astype(F32) + convolved(w_two, acts, PLANE)
    out_ref[...] = grid_one.astype(BF16)

    upstream = (pre_back[CHANNELS : CHANNELS + own_rows, TILE : TILE + PLANE], own[1])
    wide = 8 * CHANNELS
    acts[3 * rows :, :] = jnp.zeros((wide - rows, MID), BF16)
    row_plane = lax.div(lax.broadcasted_iota(jnp.int32, (own_rows, wide), 0), CHANNELS)
    col_plane = lax.div(lax.broadcasted_iota(jnp.int32, (own_rows, wide), 1), CHANNELS)
    for conv in range(2):
        for step_y in range(3):
            for step_z in range(3):
                if conv == 0:
                    start = step_z * wide
                    at = (step_y + 1) * TILE
                    field = zeros[start : start + wide, at : at + PLANE]
                else:
                    at = step_y * TILE
                    start = step_z * rows
                    field = acts[start : start + wide, at : at + PLANE]
                product = lax.dot_general(upstream[conv], field, NT, preferred_element_type=F32)
                for step_x in range(3):
                    kept = jnp.where(col_plane == row_plane + (step_x + 1 - conv), product, 0.0)
                    folded = kept[:CHANNELS]
                    for x in range(1, CXD):
                        folded = folded + kept[x * CHANNELS : (x + 1) * CHANNELS]
                    at = (conv * 27 + step_x * 9 + step_y * 3 + step_z) * CHANNELS
                    reduced[at : at + CHANNELS, :] = folded[:, :128] + folded[:, 128:]
    quarter = 2 * 27 * CHANNELS // 4
    lane_group = lax.div(lax.broadcasted_iota(jnp.int32, (quarter, 128), 1), CHANNELS)
    total = None
    for part in range(4):
        summed = reduced[part * quarter : (part + 1) * quarter, :]
        summed = summed + pltpu.roll(summed, 2 * CHANNELS, 1)
        summed = summed + pltpu.roll(summed, CHANNELS, 1)
        total = summed if total is None else jnp.where(lane_group == part, summed, total)
    small = small_ref[...]
    filler = jnp.zeros((4 * DEVICES - quarter - small.shape[0], SLOTS), F32)
    grads_ref[:quarter] = total
    grads_ref[quarter:] = jnp.concatenate([small, filler], axis=0)


def band(kernel, planes):
    taps = kernel.reshape(3, 3, 3, CHANNELS, CHANNELS)
    taps = jnp.transpose(taps, (1, 3, 2, 0, 4))
    taps = jnp.pad(taps, ((0, 0), (0, 0), (0, 0), (0, planes - 1), (0, 0)))
    return taps.reshape(3, CHANNELS, 3 * (planes + 2) * CHANNELS)


def toeplitz_kernel(*refs):
    for band_ref, out_ref in zip(refs[:4], refs[4:]):
        for step in range(3):
            first = band_ref[step].astype(F32)
            for x in range(out_ref.shape[1] // CHANNELS):
                moved = first if x == 0 else pltpu.roll(first, x * CHANNELS, 1)
                out_ref[step, x * CHANNELS : (x + 1) * CHANNELS, :] = moved.astype(BF16)


def toeplitz(kernel_one, kernel_two):
    bands = (
        band(kernel_one, 6),
        band(flipped(kernel_two), 6),
        band(kernel_two, 4),
        band(flipped(kernel_one), 4),
    )
    return pl.pallas_call(
        toeplitz_kernel,
        out_shape=[
            jax.ShapeDtypeStruct((3, planes * CHANNELS, 3 * (planes + 2) * CHANNELS), BF16)
            for planes in (6, 6, 4, 4)
        ],
        compiler_params=params(10),
        cost_estimate=cost(10**7, 4 * 2**20),
    )(*bands)


def conv_block(grids, edges, weights, small):
    rows_one = 3 * 8 * CHANNELS
    rows_two = 3 * 6 * CHANNELS
    shape = jax.ShapeDtypeStruct((CXD * CHANNELS, PLANE), BF16)
    return pl.pallas_call(
        conv_kernel,
        out_shape=(
            shape,
            jax.ShapeDtypeStruct((6 * CHANNELS, MID), BF16),
            jax.ShapeDtypeStruct((4 * DEVICES, SLOTS), F32),
        ),
        scratch_shapes=[
            pltpu.VMEM((rows_one, WIDE), BF16),
            pltpu.VMEM((rows_one, WIDE), BF16),
            pltpu.VMEM((rows_two + 2 * CHANNELS, MID), BF16),
            pltpu.VMEM((2 * 27 * CHANNELS, 128), F32),
        ],
        compiler_params=params(28),
        cost_estimate=cost(6 * 10**9, 8 * 2**20),
    )(grids, *edges, *weights[:3], small)


def last_kernel(own, pre_ref, w_last, out_ref, pres):
    shifted(pre_ref[...], pres)
    out_ref[...] = (own[0].astype(F32) + convolved(w_last, pres, PLANE)).astype(BF16)


def last_conv(grids, pre_back, weight):
    rows = CXD * CHANNELS
    return pl.pallas_call(
        last_kernel,
        grid=(1,),
        in_specs=[
            pl.BlockSpec((1, rows, PLANE), lambda i: (1, 0, 0)),
            pl.BlockSpec(pre_back.shape, lambda i: (0, 0)),
            pl.BlockSpec(weight.shape, lambda i: (0, 0, 0)),
        ],
        out_specs=pl.BlockSpec((rows, PLANE), lambda i: (0, 0)),
        out_shape=jax.ShapeDtypeStruct((rows, PLANE), BF16),
        scratch_shapes=[pltpu.VMEM((3 * 6 * CHANNELS, MID), BF16)],
        compiler_params=params(10),
        cost_estimate=cost(10**9, 2 * 2**20),
    )(grids, pre_back, weight)


def unroute_kernel(ret_ref, slot_ref, owner_ref, local_ref, out_ref, *refs):
    rows = CHANNELS
    table = refs[-1]
    for high in range(HIGH):
        for low in range(LOW):
            table[low * rows : (low + 1) * rows, high * SLOTS : (high + 1) * SLOTS] = ret_ref[
                high * LOW + low, :rows, :
            ]
    width = 512
    for step in range(PARTICLES // width):
        lanes = slice(step * width, (step + 1) * width)
        slot_ids = lax.broadcasted_iota(jnp.int32, (HIGH * SLOTS, width), 0)
        hot = (slot_ids == slot_ref[:, lanes]).astype(F32).astype(BF16)
        found = jnp.dot(table[...], hot, preferred_element_type=F32)
        low = lax.rem(owner_ref[:, lanes], LOW)
        mine = None
        for group in range(LOW):
            part = jnp.where(low == group, found[group * rows : (group + 1) * rows], 0.0)
            mine = part if mine is None else mine + part
        out_ref[:, lanes] = (mine + local_ref[:, lanes]).astype(BF16)
    if len(refs) == 1:
        return

    kernels_ref, in_ref, mlp_ref = refs[:3]
    halves = ret_ref[:, rows:, :].astype(F32)
    summed = (halves + pltpu.roll(halves, 4, 1)).reshape(DEVICES // 2, 2, 8, SLOTS)
    upper = lax.broadcasted_iota(jnp.int32, (DEVICES // 2, 8, SLOTS), 1) < 4
    summed = jnp.where(upper, summed[:, 0], summed[:, 1]).reshape(4 * DEVICES, SLOTS)
    quarter = 2 * 27 * CHANNELS // 4
    for part in range(4):
        turned = summed[:quarter]
        if part:
            turned = pltpu.roll(turned, 128 - part * CHANNELS, 1)
        kernels_ref[part * quarter : (part + 1) * quarter, :] = turned[:, :CHANNELS]
    in_ref[...] = summed[quarter : quarter + CHANNELS]
    mlp_ref[...] = summed[quarter + CHANNELS : quarter + 2 * CHANNELS]


def unroute(returned, slot, owner, addend, sums):
    shapes = [jax.ShapeDtypeStruct((CHANNELS, PARTICLES), BF16)]
    if sums:
        shapes += [
            jax.ShapeDtypeStruct((2 * 27 * CHANNELS, CHANNELS), F32),
            jax.ShapeDtypeStruct((CHANNELS, 128), F32),
            jax.ShapeDtypeStruct((CHANNELS, 128), F32),
        ]
    return pl.pallas_call(
        unroute_kernel,
        out_shape=shapes,
        scratch_shapes=[pltpu.VMEM((LOW * CHANNELS, HIGH * SLOTS), BF16)],
        compiler_params=params(14),
        cost_estimate=cost(512 * 1024 * PARTICLES, 3 * 2**20),
    )(returned, slot, owner, addend)


def exchanged(blocks):
    return lax.all_to_all(blocks, ("aa", "ba"), split_axis=0, concat_axis=0, tiled=True)


def local(features, cotangent, owner, offset, kernel_one, kernel_two, mlp_in, mlp_out):
    owner = owner.reshape(1, PARTICLES)
    outgoing, slot = route(owner, features, cotangent, offset)
    arrived = exchanged(outgoing)
    local_out, local_back, small = network(features, cotangent, mlp_in, mlp_out)
    weights = toeplitz(kernel_one, kernel_two)
    arrived, weights, small = lax.optimization_barrier((arrived, weights, small))
    grids, head_x, tail_x, head_y, tail_y = scatter(arrived)
    x_low, x_high = moved(tail_x, "ba", 1), moved(head_x, "ba", -1)
    border_head, border_tail = borders(x_low, x_high, head_y, tail_y)
    y_low, y_high = moved(border_tail, "aa", 1), moved(border_head, "aa", -1)
    edges = (x_low, x_high, y_low, y_high)
    grid_one, pre_back, parts = conv_block(grids, edges, weights, small)
    first = exchanged(gather(arrived, grid_one, parts.reshape(DEVICES // 2, 8, SLOTS)))
    back_zero = last_conv(grids, pre_back, weights[3])
    second = exchanged(attach(first, gather(arrived, back_zero)))
    (particle_out,) = unroute(first, slot, owner, local_out, False)
    feat_grad, grad_kernels, grad_in, grad_out = unroute(second, slot, owner, local_back, True)
    grad_kernels = grad_kernels.reshape(2, 27, CHANNELS, CHANNELS)
    return particle_out, feat_grad, grad_kernels, grad_in.T, grad_out


def solution(mesh):
    in_specs = (
        P(None, ("aa", "ba")),
        P(None, ("aa", "ba")),
        P(("aa", "ba"), None),
        P(None, ("aa", "ba")),
        P(),
        P(),
        P(),
        P(),
    )
    out_specs = (P(None, ("aa", "ba")), P(None, ("aa", "ba")), P(), P(), P())
    return jax.shard_map(local, mesh=mesh, in_specs=in_specs, out_specs=out_specs, check_vma=False)
```
